32 devices in a mesh: ens: 2 (over x), gx: 8 (over z, y), gy: 2 (over core).
Axes of the slice: x: 2, y: 2, z: 4, core: 2. Of those that a mesh axis runs over, the one named last changes fastest.
Arguments:
- atm_fields: float32 [8, 60, 256, 256], P('ens', None, 'gx', 'gy'), parts along dimension 0, may hold values from -5 to 5
- ocean_fields: float32 [8, 40, 512, 512], P('ens', None, 'gx', 'gy'), parts along dimension 0, may hold values from -5 to 5
- land_sea: int32 [1024, 512], P(('ens', 'gx'), 'gy'), parts along dimension 0, may hold values 0 or 1
- sea_weights: float32 [768, 128, 128], P(('ens', 'gx', 'gy')), parts along dimension 0, may hold values from -0.5 to 0.5
- sea_dest: int32 [768, 1], P(('ens', 'gx', 'gy')), parts along dimension 0, may hold values from 0 to 15; in each aligned block of 24 rows (0 to 23, 24 to 47, ...) at most 2 rows name the same one
- sea_source: int32 [768], P(('ens', 'gx', 'gy')), parts along dimension 0, may hold values from 0 to 127
- sea_window: int32 [768], P(('ens', 'gx', 'gy')), parts along dimension 0, may hold values from 0 to 31
- air_weights: float32 [768, 128, 128], P(('ens', 'gx', 'gy')), parts along dimension 0, may hold values from -0.5 to 0.5
- air_dest: int32 [768, 1], P(('ens', 'gx', 'gy')), parts along dimension 0, may hold values from 0 to 15; in each aligned block of 24 rows (0 to 23, 24 to 47, ...) at most 2 rows name the same one
- air_source: int32 [768], P(('ens', 'gx', 'gy')), parts along dimension 0, may hold values from 0 to 31
- air_window: int32 [768], P(('ens', 'gx', 'gy')), parts along dimension 0, may hold values from 0 to 127
Outputs:
- air_next: float32 [4, 60, 256, 256], P('ens', None, 'gx', 'gy'), parts along dimension 0
- sea_next: float32 [4, 40, 512, 512], P('ens', None, 'gx', 'gy'), parts along dimension 0
The draws below stay inside these ranges and needn't reach their ends.
There are 2 independent parts, one for each index of `ens`. The reference program is written for one: setup_inputs(seed, part) draws one part's arguments, and reference() takes and returns one part's arrays. A program takes and returns all parts, laid end to end along the dimension named above; each array names one. Nothing has to cross between parts.
Inputs may be any that keep to these rules, and one draw needn't show every extreme that they name: `sea_dest`: in each aligned block of 24 rows (the blocks of one source tile) no tile is named by more than 2 rows; some block names one tile exactly 2 times. `air_dest`: in each aligned block of 24 rows (the blocks of one source tile) no tile is named by more than 2 rows; some block names one tile exactly 2 times.
All inputs are finite; a program needn't handle non-finite values. No bound on the sum of `land_sea` on one device may be relied on, other than what follows from the above.
Results may differ from the reference program's by a relative error of at most 0.000071.
Values sent between devices are 32-bit elements; how exact they have to be, the bound alone decides.
No kernel may reach another device: no remote copies, remote signals or barrier semaphores. Data moves between devices by JAX's collectives and lax.ppermute only.
A program may use at most 192 MiB of HBM per device.

```python
import math
import jax
import jax.numpy as jnp
import numpy as np
from jax import lax

LA = 60
LO = 40
ACX = 32
ACY = 128
OCX = 64
OCY = 256
WIN = 128
NB = 24
CAP = 2
TILES = 16
SLOTS = 384
AX = 256
AY = 256
OX = 512
OY = 512
AWIN = 32
OWIN = 128
N_GX = 8
N_GY = 2


def set_ends(drawn, own_key, least, high):
    extent = drawn.shape
    index_at = [jax.random.randint(jax.random.fold_in(own_key, axis), (), 0, extent[axis]) for axis in range(len(extent))]
    drawn = drawn.at[tuple(index_at)].set(least)
    longest = extent.index(max(extent))
    index_at[longest] = (index_at[longest] + 1) % extent[longest]
    return drawn.at[tuple(index_at)].set(high)


def block_scale(rng, shape, split, smallest, high):
    gain = 1.0
    for position, blocks in split:
        draws = jax.random.uniform(jax.random.fold_in(jax.random.fold_in(rng, 6), position), (blocks,), jnp.float32, smallest / len(split), high / len(split))
        gain = gain * jnp.repeat(jnp.exp(draws), shape[position] // blocks).reshape((-1,) + (1,) * (len(shape) - 1 - position))
    return gain


def assign_block(rng, own, number, rows, number_of, top, reach, skew):
    order = jax.random.permutation(rng, number_of)
    heavy_load, common = shares(number_of, rows * top, reach, skew, True), shares(number_of, rows * top, reach, skew, False)
    places = jnp.arange(number_of)

    def named(sizes, turn):
        used = int((sizes > 0).sum())
        fixed = max(1, used // 4)
        passed = fixed + (places - fixed + turn * (used - fixed)) % max(1, number_of - fixed)
        return jnp.zeros((number_of,), jnp.int32).at[order[jnp.where(places < fixed, places, passed)]].set(jnp.asarray(sizes, jnp.int32))

    sizes = jnp.where(number % 4 == 0, named(heavy_load, number // 4), named(common, number - number // 4 - 1))
    mixed = jax.random.permutation(jax.random.fold_in(own, 3), number_of)
    giver, sink = mixed[0:number_of // 2 * 2:2], mixed[1:number_of // 2 * 2:2]
    slack = jnp.minimum(sizes[giver] - 1, reach - sizes[sink]) // 2
    slack = jnp.where((giver == order[0]) | (sink == order[0]) | (sizes[sink] == 0), 0, jnp.maximum(slack, 0))
    passed = jax.random.randint(jax.random.fold_in(own, 4), (number_of // 2,), 0, 1 << 20) % (slack + 1)
    sizes = sizes.at[giver].add(-passed).at[sink].add(passed)
    labels = jnp.searchsorted(jnp.cumsum(sizes), jnp.arange(rows * top), side="right").astype(jnp.int32)
    grid = labels.reshape(top, rows).T
    grid = grid[jax.random.permutation(jax.random.fold_in(own, 1), rows)]
    turn = jax.random.randint(jax.random.fold_in(own, 2), (rows, 1), 0, top)
    return jnp.take_along_axis(grid, (jnp.arange(top)[None, :] + turn) % top, axis=1)


def shares(number_of, total, bound, skew, full):
    weights = [(1 << 20) // math.isqrt(rank ** skew) + 1 for rank in range(1, number_of + 1)]
    largest = bound if full else min(bound, max(-(-total // number_of), total * weights[0] // sum(weights)))
    least = 1 if total - largest >= number_of - 1 else 0
    given, rest = [largest] + [least] * (number_of - 1), total - largest - least * (number_of - 1)
    while rest > 0:
        movable = [i for i in range(1, number_of) if given[i] < largest] or [i for i in range(1, number_of) if given[i] < bound]
        whole, budget = sum([weights[i] for i in movable]), rest
        for i in movable:
            extra = min(bound - given[i], max(1, budget * weights[i] // whole), rest)
            given[i] = given[i] + extra
            rest = rest - extra
    return np.array(given)


def normal_values(own_key, shape, width, reach, cuts=(), held_as=jnp.bfloat16):
    drawn = jax.random.normal(own_key, shape, jnp.float32) * width
    if len(cuts) > 0:
        drawn = block_scale(own_key, shape, cuts, -0.22, 0.18) * drawn
    return jnp.clip(drawn, min=-reach, max=reach).astype(held_as)


def setup_inputs(seed: int = 0, part: int = 0) -> dict:
    keys = jax.random.split(jax.random.key(seed), 12)
    part_keys = jax.random.split(jax.random.fold_in(keys[11], part), 12)
    atm_fields = normal_values(part_keys[0], (4, LA, AX, AY), 1.0, 5.0, ((2, 8), (3, 2)), jnp.float32)
    ocean_fields = normal_values(part_keys[1], (4, LO, OX, OY), 1.0, 5.0, ((2, 8), (3, 2)), jnp.float32)
    land_sea = set_ends((jax.random.randint(part_keys[2], (OX, OY), 0, 4) < 3).astype(jnp.int32), jax.random.fold_in(part_keys[2], 1), 0, 1)
    sea_weights = normal_values(part_keys[3], (SLOTS, WIN, WIN), WIN ** -0.5, 0.5, ((0, 16),), jnp.float32)
    sea_dest_keys = jax.random.split(jax.random.fold_in(part_keys[4], 1), SLOTS // NB)
    sea_dest_turns = jax.random.permutation(jax.random.fold_in(part_keys[4], 3), SLOTS // NB)
    sea_dest = jax.vmap(lambda own, number: assign_block(jax.random.fold_in(part_keys[4], 2), own, number, NB, TILES, 1, CAP, 2))(sea_dest_keys, sea_dest_turns).reshape((SLOTS, 1))
    sea_source = set_ends(jax.random.randint(part_keys[5], (SLOTS,), 0, OWIN), jax.random.fold_in(part_keys[5], 1), 0, OWIN - 1).astype(jnp.int32)
    sea_window = set_ends(jax.random.randint(part_keys[6], (SLOTS,), 0, AWIN), jax.random.fold_in(part_keys[6], 1), 0, AWIN - 1).astype(jnp.int32)
    air_weights = normal_values(part_keys[7], (SLOTS, WIN, WIN), WIN ** -0.5, 0.5, ((0, 16),), jnp.float32)
    air_dest_keys = jax.random.split(jax.random.fold_in(part_keys[8], 1), SLOTS // NB)
    air_dest_turns = jax.random.permutation(jax.random.fold_in(part_keys[8], 3), SLOTS // NB)
    air_dest = jax.vmap(lambda own, number: assign_block(jax.random.fold_in(part_keys[8], 2), own, number, NB, TILES, 1, CAP, 2))(air_dest_keys, air_dest_turns).reshape((SLOTS, 1))
    air_source = set_ends(jax.random.randint(part_keys[9], (SLOTS,), 0, AWIN), jax.random.fold_in(part_keys[9], 1), 0, AWIN - 1).astype(jnp.int32)
    air_window = set_ends(jax.random.randint(part_keys[10], (SLOTS,), 0, OWIN), jax.random.fold_in(part_keys[10], 1), 0, OWIN - 1).astype(jnp.int32)
    return dict(atm_fields=atm_fields, ocean_fields=ocean_fields, land_sea=land_sea, sea_weights=sea_weights, sea_dest=sea_dest, sea_source=sea_source, sea_window=sea_window, air_weights=air_weights, air_dest=air_dest, air_source=air_source, air_window=air_window)


precise = lax.Precision.HIGHEST
time_step = 0.1
diffusion = 0.2

def step_cells(padded, east_flow, north_flow, forcing):
    along_x = padded[:, :, :, 1:-1]
    along_y = padded[:, :, 1:-1, :]
    centre = along_x[:, :, 1:-1]
    face_x = 0.25 * (east_flow[:, :-1] + east_flow[:, 1:])[None] * (along_x[:, :, :-1] + along_x[:, :, 1:])
    face_y = 0.25 * (north_flow[:, :, :-1] + north_flow[:, :, 1:])[None] * (along_y[:, :, :, :-1] + along_y[:, :, :, 1:])
    spread = along_x[:, :, 2:] + along_x[:, :, :-2] + along_y[:, :, :, 2:] + along_y[:, :, :, :-2] - 4.0 * centre
    tendency = diffusion * spread - (face_x[:, :, 1:] - face_x[:, :, :-1]) - (face_y[:, :, :, 1:] - face_y[:, :, :, :-1])
    updated = centre + time_step * tendency
    return updated.at[:, 0].add(time_step * forcing)

def advance_whole(fields, forcing):
    padded = jnp.pad(fields, ((0, 0), (0, 0), (1, 1), (1, 1)))
    return step_cells(padded[:2], padded[2][:, :, 1:-1], padded[3][:, 1:-1, :], forcing)

def regrid_whole(fields, source_win, dest_tile, dest_win, weights, src_rows, src_cols, dst_rows, dst_cols):
    nfield = fields.shape[0]
    blocks = fields.reshape(nfield, N_GX, src_rows, N_GY, src_cols).transpose(1, 3, 0, 2, 4)
    blocks = blocks.reshape(TILES, nfield, src_rows * src_cols // WIN, WIN)
    chosen = source_win.reshape(TILES, NB)
    picked = blocks[jnp.arange(TILES, dtype=jnp.int32)[:, None], :, chosen]
    values = jnp.einsum('tkab,tkfb->tkfa', weights.reshape(TILES, NB, WIN, WIN), picked, precision=precise)
    windows = dst_rows * dst_cols // WIN
    target = (dest_tile[:, 0] * windows + dest_win).astype(jnp.int32)
    summed = jnp.zeros((TILES * windows, nfield, WIN), jnp.float32).at[target].add(values.reshape(TILES * NB, nfield, WIN))
    summed = summed.reshape(N_GX, N_GY, windows, nfield, WIN).transpose(3, 0, 1, 2, 4)
    summed = summed.reshape(nfield, N_GX, N_GY, dst_rows, dst_cols).transpose(0, 1, 3, 2, 4)
    return summed.reshape(nfield, N_GX * dst_rows, N_GY * dst_cols)

def bulk_fluxes(atm_fields, on_air):
    relative_u = atm_fields[2, 0] - on_air[1]
    relative_v = atm_fields[3, 0] - on_air[2]
    wind_speed = jnp.sqrt(relative_u * relative_u + relative_v * relative_v + 1.0)
    heat_flux = 0.5 * wind_speed * (on_air[0] - atm_fields[0, 0])
    moisture = 0.4 * wind_speed * (0.8 * on_air[0] - atm_fields[1, 0])
    return jnp.stack((heat_flux, moisture))

def reference(atm_fields, ocean_fields, land_sea, sea_weights, sea_dest, sea_source, sea_window, air_weights, air_dest, air_source, air_window):
    surface = jnp.stack((ocean_fields[0, 0], ocean_fields[2, 0], ocean_fields[3, 0]))
    on_air = regrid_whole(surface, sea_source, sea_dest, sea_window, sea_weights, OCX, OCY, ACX, ACY)
    fluxes = bulk_fluxes(atm_fields, on_air)
    air_next = advance_whole(atm_fields, fluxes)
    on_sea = regrid_whole(fluxes, air_source, air_dest, air_window, air_weights, ACX, ACY, OCX, OCY)
    sea_forcing = jnp.stack((-0.5 * on_sea[0], 0.3 * on_sea[1]))
    sea_step = advance_whole(ocean_fields, sea_forcing)
    sea_next = jnp.where(land_sea[None, None] == 1, sea_step, ocean_fields[:2])
    return (air_next, sea_next)
```

```python
import functools

import jax
import jax.numpy as jnp
from jax import lax
from jax.experimental import pallas as pl
from jax.experimental.pallas import tpu as pltpu
from jax.sharding import PartitionSpec as P

WIN = 128
CAP = 2
ROWS = 4
LANES = 128
SUB = 8

time_step = 0.1
diffusion = 0.2
VMEM_LIMIT = 56 * 1024 * 1024


def lane_of(shape):
    return lax.broadcasted_iota(jnp.int32, shape, len(shape) - 1)


def row_of(shape):
    return lax.broadcasted_iota(jnp.int32, shape, len(shape) - 2)


def send_blocks(pick, count, weights_ref, dest_ref, window_ref, picked_ref, counts_ref, out_ref):
    blocks = weights_ref.shape[0]
    out_ref[...] = jnp.zeros_like(out_ref)

    def clear(d, carry):
        counts_ref[d] = 0
        return carry

    lax.fori_loop(0, out_ref.shape[0], clear, 0)
    picked_ref[...] = jnp.zeros_like(picked_ref)
    for k in range(blocks):
        for f in range(count):
            picked_ref[k, pl.ds(f, 1), :] = pick(k, f)
    row = row_of((SUB, LANES))
    lane = lane_of((SUB, LANES))
    for k in range(blocks):
        values = picked_ref[k]
        high = values.astype(jnp.bfloat16)
        low = (values - high.astype(jnp.float32)).astype(jnp.bfloat16)
        left = jnp.concatenate([high.astype(jnp.float32), low.astype(jnp.float32)], axis=0).astype(jnp.bfloat16)
        weight = weights_ref[k]
        weight_high = weight.astype(jnp.bfloat16)
        weight_low = (weight - weight_high.astype(jnp.float32)).astype(jnp.bfloat16)
        right = jnp.concatenate([weight_high, weight_low], axis=0)
        product = lax.dot_general(left, right, (((1,), (1,)), ((), ())), preferred_element_type=jnp.float32)
        total = product[:SUB, :WIN] + (product[SUB:, :WIN] + product[:SUB, WIN:])
        d = dest_ref[k, 0]
        slot = counts_ref[d]
        counts_ref[d] = slot + 1
        onehot = jnp.where(lane == window_ref[k], 1.0, 0.0)
        total = jnp.where(row == ROWS - 1, onehot, jnp.where(row < count, total, 0.0))
        total = jnp.where(slot == 0, total, jnp.concatenate([total[ROWS:], total[:ROWS]], axis=0))
        out_ref[d] = out_ref[d] + total


def receive_blocks(arrived_ref, count):
    slots = arrived_ref.shape[0] // ROWS
    onehot = arrived_ref[pl.ds(ROWS - 1, slots, stride=ROWS), :]
    fields = [arrived_ref[pl.ds(f, slots, stride=ROWS), :] for f in range(count)]
    return [
        lax.dot_general(
            onehot, field, (((0,), (0,)), ((), ())), precision=lax.Precision.HIGHEST, preferred_element_type=jnp.float32
        )
        for field in fields
    ]


def sea_send_kernel(
    dest_ref, source_ref, window_ref, ocean_ref, weights_ref, out_ref, picked_ref, counts_ref, surface_ref
):
    rows, cols = ocean_ref.shape[2:]
    halves = cols // WIN
    for f in range(3):
        for h in range(halves):
            surface_ref[f, pl.ds(h, rows, stride=halves), :] = ocean_ref[(0, 2, 3)[f], 0, :, pl.ds(h * WIN, WIN)]

    def pick(k, f):
        return surface_ref[f, pl.ds(source_ref[k], 1), :]

    send_blocks(pick, 3, weights_ref, dest_ref, window_ref, picked_ref, counts_ref, out_ref)


def sea_send(tiles, ocean, weights, dest, source, window):
    blocks = weights.shape[0]
    smem = pl.BlockSpec(memory_space=pltpu.SMEM)
    return pl.pallas_call(
        sea_send_kernel,
        grid=(1,),
        out_shape=jax.ShapeDtypeStruct((tiles, CAP * ROWS, WIN), jnp.float32),
        in_specs=[
            smem,
            smem,
            smem,
            pl.BlockSpec((4, 1) + ocean.shape[2:], lambda i: (0, 0, 0, 0)),
            pl.BlockSpec(weights.shape, lambda i: (0, 0, 0)),
        ],
        out_specs=pl.BlockSpec((tiles, CAP * ROWS, WIN), lambda i: (0, 0, 0)),
        scratch_shapes=[
            pltpu.VMEM((blocks, SUB, WIN), jnp.float32),
            pltpu.SMEM((tiles,), jnp.int32),
            pltpu.VMEM((3, ocean.shape[2] * ocean.shape[3] // WIN, WIN), jnp.float32),
        ],
        compiler_params=pltpu.CompilerParams(vmem_limit_bytes=VMEM_LIMIT),
        cost_estimate=pl.CostEstimate(flops=blocks * 2 * 16 * 128 * 256, bytes_accessed=2000000, transcendentals=0),
        name="sea_send",
    )(dest, source, window, ocean, weights)


def air_send_kernel(
    dest_ref, source_ref, window_ref, arrived_ref, atm_ref, weights_ref, out_ref, flux_ref, picked_ref, counts_ref
):
    rows = atm_ref.shape[2]
    on_air = [field[:rows] for field in receive_blocks(arrived_ref, 3)]
    relative_u = atm_ref[2, 0] - on_air[1]
    relative_v = atm_ref[3, 0] - on_air[2]
    wind_speed = jnp.sqrt(relative_u * relative_u + relative_v * relative_v + 1.0)
    flux_ref[0] = 0.5 * wind_speed * (on_air[0] - atm_ref[0, 0])
    flux_ref[1] = 0.4 * wind_speed * (0.8 * on_air[0] - atm_ref[1, 0])

    def pick(k, f):
        return flux_ref[f, pl.ds(source_ref[k], 1), :]

    send_blocks(pick, 2, weights_ref, dest_ref, window_ref, picked_ref, counts_ref, out_ref)


def air_send(arrived, atm, weights, dest, source, window):
    blocks = weights.shape[0]
    tiles = arrived.shape[0]
    rows, cols = atm.shape[2:]
    smem = pl.BlockSpec(memory_space=pltpu.SMEM)
    return pl.pallas_call(
        air_send_kernel,
        grid=(1,),
        out_shape=(
            jax.ShapeDtypeStruct((tiles, CAP * ROWS, WIN), jnp.float32),
            jax.ShapeDtypeStruct((2, rows, cols), jnp.float32),
        ),
        in_specs=[
            smem,
            smem,
            smem,
            pl.BlockSpec((tiles * CAP * ROWS, WIN), lambda i: (0, 0)),
            pl.BlockSpec((4, 1, rows, cols), lambda i: (0, 0, 0, 0)),
            pl.BlockSpec(weights.shape, lambda i: (0, 0, 0)),
        ],
        out_specs=(
            pl.BlockSpec((tiles, CAP * ROWS, WIN), lambda i: (0, 0, 0)),
            pl.BlockSpec((2, rows, cols), lambda i: (0, 0, 0)),
        ),
        scratch_shapes=[pltpu.VMEM((blocks, SUB, WIN), jnp.float32), pltpu.SMEM((tiles,), jnp.int32)],
        compiler_params=pltpu.CompilerParams(vmem_limit_bytes=VMEM_LIMIT),
        cost_estimate=pl.CostEstimate(flops=blocks * 2 * 16 * 128 * 256, bytes_accessed=2000000, transcendentals=0),
        name="air_send",
    )(dest, source, window, arrived.reshape(tiles * CAP * ROWS, WIN), atm, weights)


def sea_forcing_kernel(arrived_ref, land_ref, before_ref, after_ref, summed_ref):
    rows, cols = land_ref.shape
    halves = cols // WIN
    for f, field in enumerate(receive_blocks(arrived_ref, 2)):
        summed_ref[f] = field
        for h in range(halves):
            span = pl.ds(h * WIN, WIN)
            forcing = summed_ref[f, pl.ds(h, rows, stride=halves), :] * (-0.5, 0.3)[f]
            change = jnp.where(land_ref[:, span] == 1, time_step * forcing, 0.0)
            after_ref[f, 0, :, span] = before_ref[f, 0, :, span] + change


def add_sea_forcing(arrived, land, sea_next):
    tiles = arrived.shape[0]
    rows, cols = land.shape
    return pl.pallas_call(
        sea_forcing_kernel,
        grid=(1,),
        out_shape=jax.ShapeDtypeStruct(sea_next.shape, jnp.float32),
        in_specs=[
            pl.BlockSpec((tiles * CAP * ROWS, WIN), lambda i: (0, 0)),
            pl.BlockSpec((rows, cols), lambda i: (0, 0)),
            pl.BlockSpec((2, 1, rows, cols), lambda i: (0, 0, 0, 0)),
        ],
        out_specs=pl.BlockSpec((2, 1, rows, cols), lambda i: (0, 0, 0, 0)),
        scratch_shapes=[pltpu.VMEM((2, rows * cols // WIN, WIN), jnp.float32)],
        input_output_aliases={2: 0},
        compiler_params=pltpu.CompilerParams(vmem_limit_bytes=VMEM_LIMIT),
        cost_estimate=pl.CostEstimate(flops=4000000, bytes_accessed=600000, transcendentals=0),
        name="sea_forcing",
    )(arrived.reshape(tiles * CAP * ROWS, WIN), land, sea_next)


STEPS = 5


def padded_levels(levels):
    return -(-levels // SUB) * SUB


def edges_kernel(gy_ref, atm_ref, half_q_ref, half_v_ref, low_ref, high_ref, xlow_ref, xhigh_ref, y_ref):
    step = pl.program_id(0)
    air_levels, air_rows = atm_ref.shape[1:3]
    sea_levels, sea_rows = half_q_ref.shape[1:3]
    all_air, all_sea = air_levels * STEPS, sea_levels * STEPS
    halves = low_ref.shape[3] // WIN
    pitch = padded_levels(all_air)

    @pl.when(step == 0)
    def _():
        xlow_ref[...] = jnp.zeros_like(xlow_ref)
        xhigh_ref[...] = jnp.zeros_like(xhigh_ref)
        y_ref[...] = jnp.zeros_like(y_ref)

    for f in range(3):
        for level in range(air_levels):
            to = pl.ds(f * pitch + step * air_levels + level, 1)
            xlow_ref[to, :] = atm_ref[f, level, pl.ds(0, 1), :]
            xhigh_ref[to, :] = atm_ref[f, level, pl.ds(air_rows - 1, 1), :]
        for h in range(halves):
            for level in range(sea_levels):
                to = pl.ds(3 * pitch + (f * halves + h) * all_sea + step * sea_levels + level, 1)
                span = pl.ds(h * WIN, WIN)
                xlow_ref[to, :] = low_ref[f, level, pl.ds(0, 1), span]
                xhigh_ref[to, :] = high_ref[f, level, pl.ds(SUB - 1, 1), span]

    edge = jnp.where(gy_ref[0] == 0, LANES - 1, 0)

    def put(total, column, to, lane):
        return jnp.where(lane == to, pltpu.roll(column, (to - edge + LANES) % LANES, 1), total)

    lane = lane_of((air_rows, LANES))
    tracers, v = y_ref[:air_rows], y_ref[air_rows : 2 * air_rows]
    for level in range(air_levels):
        to = step * air_levels + level
        tracers = put(tracers, atm_ref[0, level], to, lane)
        tracers = put(tracers, atm_ref[1, level], LANES // 2 + to, lane)
        v = put(v, atm_ref[3, level], to, lane)
    y_ref[:air_rows] = tracers
    y_ref[air_rows : 2 * air_rows] = v
    lane = lane_of((sea_rows, LANES))
    total = y_ref[2 * air_rows :]
    for level in range(sea_levels):
        to = step * sea_levels + level
        total = put(total, half_q_ref[0, level], to, lane)
        total = put(total, half_q_ref[1, level], all_sea + to, lane)
        total = put(total, half_v_ref[0, level], 2 * all_sea + to, lane)
    y_ref[2 * air_rows :] = total


def edges(gy, atm, ocean):
    air_levels, air_rows, _ = atm.shape[1:]
    sea_levels, sea_rows, sea_cols = ocean.shape[1:]
    a, o = air_levels // STEPS, sea_levels // STEPS
    xrows = 3 * padded_levels(air_levels) + 3 * sea_levels * (sea_cols // WIN)
    yrows = 2 * air_rows + sea_rows
    last = sea_cols // WIN - 1
    x_shape = jax.ShapeDtypeStruct((xrows, LANES), jnp.float32)
    return pl.pallas_call(
        edges_kernel,
        grid_spec=pltpu.PrefetchScalarGridSpec(
            num_scalar_prefetch=1,
            grid=(STEPS,),
            in_specs=[
                pl.BlockSpec((4, a, air_rows, LANES), lambda i, gy: (0, i, 0, 0)),
                pl.BlockSpec((2, o, sea_rows, LANES), lambda i, gy: (0, i, 0, last * (1 - gy[0]))),
                pl.BlockSpec((1, o, sea_rows, LANES), lambda i, gy: (3, i, 0, last * (1 - gy[0]))),
                pl.BlockSpec((3, o, SUB, sea_cols), lambda i, gy: (0, i, 0, 0)),
                pl.BlockSpec((3, o, SUB, sea_cols), lambda i, gy: (0, i, sea_rows // SUB - 1, 0)),
            ],
            out_specs=[
                pl.BlockSpec((xrows, LANES), lambda i, gy: (0, 0)),
                pl.BlockSpec((xrows, LANES), lambda i, gy: (0, 0)),
                pl.BlockSpec((yrows, LANES), lambda i, gy: (0, 0)),
            ],
        ),
        out_shape=(x_shape, x_shape, jax.ShapeDtypeStruct((yrows, LANES), jnp.float32)),
        compiler_params=pltpu.CompilerParams(vmem_limit_bytes=VMEM_LIMIT),
        cost_estimate=pl.CostEstimate(flops=2000000, bytes_accessed=10000000, transcendentals=0),
        name="edges",
    )(gy, atm, ocean, ocean, ocean, ocean)


def step_level(fields, west, east, south, write):
    row = row_of((SUB, LANES))
    lane = lane_of((SUB, LANES))
    groups, halves = fields.groups, fields.halves
    first_row, last_row = row == 0, row == SUB - 1
    first_lane, last_lane = lane == 0, lane == LANES - 1

    def along_x(f, h, scale):
        tiles = [fields(f, r, h) for r in range(groups)]
        if scale is not None:
            tiles = [scale * t for t in tiles]
        down = [pltpu.roll(t, 1, 0) for t in tiles]
        up = [pltpu.roll(t, SUB - 1, 0) for t in tiles]
        before = [jnp.broadcast_to(west(f, h), (SUB, LANES))] + down[:-1]
        after = up[1:] + [jnp.broadcast_to(east(f, h), (SUB, LANES))]
        if scale is not None:
            before[0], after[-1] = scale * before[0], scale * after[-1]
        lows = [jnp.where(first_row, b, d) for b, d in zip(before, down)]
        highs = [jnp.where(last_row, a, u) for a, u in zip(after, up)]
        return tiles, lows, highs

    def along_y(f, r, tiles, scale):
        beyond = south(f, r)
        if scale is not None:
            beyond = scale * beyond
        right = [pltpu.roll(t, 1, 1) for t in tiles]
        left = [pltpu.roll(t, LANES - 1, 1) for t in tiles]
        lows = [jnp.where(first_lane, b, t) for b, t in zip([beyond] + right[:-1], right)]
        highs = [jnp.where(last_lane, b, t) for b, t in zip(left[1:] + [beyond], left)]
        return lows, highs

    scale = 0.25 * time_step
    mixing = time_step * diffusion
    moved = [[along_x(f, h, scale if f == 2 else None) for h in range(halves)] for f in range(3)]
    for r in range(groups):
        v = [scale * fields(3, r, h) for h in range(halves)]
        v_low, v_high = along_y(3, r, v, scale)
        sides = [along_y(f, r, [moved[f][h][0][r] for h in range(halves)], None) for f in range(2)]
        for h in range(halves):
            u, u_low, u_high = (part[r] for part in moved[2][h])
            centre = (1.0 - 4.0 * mixing) + ((u_low - u_high) + (v_low[h] - v_high[h]))
            x_high, x_low = (mixing - u) - u_high, (mixing + u) + u_low
            y_high, y_low = (mixing - v[h]) - v_high[h], (mixing + v[h]) + v_low[h]
            for f in range(2):
                q, q_low, q_high = (part[r] for part in moved[f][h])
                new = centre * q + (x_high * q_high + x_low * q_low)
                new = new + (y_high * sides[f][1][h] + y_low * sides[f][0][h])
                write(f, r, h, new, q)


class Fields:
    def __init__(self, ref, level):
        self.ref, self.level = ref, level
        self.groups, self.halves = ref.shape[2] // SUB, ref.shape[3] // LANES

    def __call__(self, f, r, h):
        return self.ref[f, self.level, pl.ds(r * SUB, SUB), pl.ds(h * LANES, LANES)]


def transport_kernel(gy_ref, atm_ref, ocean_ref, land_ref, flux_ref, xlow_ref, xhigh_ref, y_ref, air_ref, sea_ref):
    step = pl.program_id(0)
    steps = pl.num_programs(0)
    air_levels, air_rows = atm_ref.shape[1:3]
    sea_levels, sea_rows, sea_cols = ocean_ref.shape[1:]
    all_air, all_sea = STEPS_T * air_levels, STEPS_T * sea_levels
    halves = sea_cols // LANES
    pitch = padded_levels(all_air)
    edge = jnp.where(gy_ref[0] == 0, LANES - 1, 0)
    at_edge = lane_of((SUB, LANES)) == edge

    def column(start, r, at):
        tile = y_ref[pl.ds(start + r * SUB, SUB), :]
        return jnp.where(at_edge, pltpu.roll(tile, (edge - at + LANES) % LANES, 1), 0.0)

    def air_level(level, carry):
        here = step * air_levels + level

        def beyond(f, r):
            start = air_rows if f == 3 else 0
            return column(start, r, (LANES // 2 if f == 1 else 0) + here)

        def write(f, r, h, new, q):
            air_ref[f, level, pl.ds(r * SUB, SUB), :] = new

        step_level(
            Fields(atm_ref, level),
            lambda f, h: xlow_ref[pl.ds(f * pitch + here, 1), :],
            lambda f, h: xhigh_ref[pl.ds(f * pitch + here, 1), :],
            beyond,
            write,
        )
        return carry

    lax.fori_loop(0, air_levels, air_level, 0)

    @pl.when(step == 0)
    def _():
        for f in range(2):
            air_ref[f, 0] = air_ref[f, 0] + time_step * flux_ref[f]

    def sea_level(level, carry):
        here = step * sea_levels + level

        def beyond(f, r):
            return column(2 * air_rows, r, (2 if f == 3 else f) * all_sea + here)

        def write(f, r, h, new, q):
            rows, span = pl.ds(r * SUB, SUB), pl.ds(h * LANES, LANES)
            sea_ref[f, level, rows, span] = jnp.where(land_ref[rows, span] == 1, new, q)

        step_level(
            Fields(ocean_ref, level),
            lambda f, h: xlow_ref[pl.ds(3 * pitch + (f * halves + h) * all_sea + here, 1), :],
            lambda f, h: xhigh_ref[pl.ds(3 * pitch + (f * halves + h) * all_sea + here, 1), :],
            beyond,
            write,
        )
        return carry

    lax.fori_loop(0, sea_levels, sea_level, 0)


STEPS_T = 10


def transport(gy, atm, ocean, land, flux, xlow, xhigh, y):
    air_levels, air_rows, _ = atm.shape[1:]
    sea_levels, sea_rows, sea_cols = ocean.shape[1:]
    a, o = air_levels // STEPS_T, sea_levels // STEPS_T

    def whole(array):
        return pl.BlockSpec(array.shape, lambda i, gy: (0,) * array.ndim)

    return pl.pallas_call(
        transport_kernel,
        grid_spec=pltpu.PrefetchScalarGridSpec(
            num_scalar_prefetch=1,
            grid=(STEPS_T,),
            in_specs=[
                pl.BlockSpec((4, a, air_rows, LANES), lambda i, gy: (0, i, 0, 0)),
                pl.BlockSpec((4, o, sea_rows, sea_cols), lambda i, gy: (0, i, 0, 0)),
                whole(land),
                whole(flux),
                whole(xlow),
                whole(xhigh),
                whole(y),
            ],
            out_specs=[
                pl.BlockSpec((2, a, air_rows, LANES), lambda i, gy: (0, i, 0, 0)),
                pl.BlockSpec((2, o, sea_rows, sea_cols), lambda i, gy: (0, i, 0, 0)),
            ],
        ),
        out_shape=(
            jax.ShapeDtypeStruct((2,) + atm.shape[1:], jnp.float32),
            jax.ShapeDtypeStruct((2,) + ocean.shape[1:], jnp.float32),
        ),
        compiler_params=pltpu.CompilerParams(vmem_limit_bytes=VMEM_LIMIT),
        cost_estimate=pl.CostEstimate(flops=60000000, bytes_accessed=22000000, transcendentals=0),
        name="transport",
    )(gy, atm, ocean, land, flux, xlow, xhigh, y)


def body(
    atm_fields,
    ocean_fields,
    land_sea,
    sea_weights,
    sea_dest,
    sea_source,
    sea_window,
    air_weights,
    air_dest,
    air_source,
    air_window,
):
    width_x, width_y = lax.axis_size("gx"), lax.axis_size("gy")
    assert width_y == 2
    tiles = width_x * width_y
    gy = lax.axis_index("gy").astype(jnp.int32).reshape(1)
    exchange = functools.partial(lax.all_to_all, axis_name=("gx", "gy"), split_axis=0, concat_axis=0, tiled=True)
    forward = [(i, i + 1) for i in range(width_x - 1)]
    backward = [(i + 1, i) for i in range(width_x - 1)]

    to_air = sea_send(tiles, ocean_fields, sea_weights, sea_dest, sea_source, sea_window)
    on_air = exchange(to_air)
    low, high, side = edges(gy, atm_fields, ocean_fields)
    side = lax.ppermute(side, "gy", [(0, 1), (1, 0)])
    xlow = lax.ppermute(high, "gx", forward)
    xhigh = lax.ppermute(low, "gx", backward)
    to_sea, fluxes = air_send(on_air, atm_fields, air_weights, air_dest, air_source, air_window)
    on_sea = exchange(to_sea)
    air_next, sea_next = transport(gy, atm_fields, ocean_fields, land_sea, fluxes, xlow, xhigh, side)
    sea_next = add_sea_forcing(on_sea, land_sea, sea_next)
    return (air_next, sea_next)


def solution(mesh):
    placed = (
        P("ens", None, "gx", "gy"),
        P("ens", None, "gx", "gy"),
        P(("ens", "gx"), "gy"),
        P(("ens", "gx", "gy"), None, None),
        P(("ens", "gx", "gy"), None),
        P(("ens", "gx", "gy")),
        P(("ens", "gx", "gy")),
        P(("ens", "gx", "gy"), None, None),
        P(("ens", "gx", "gy"), None),
        P(("ens", "gx", "gy")),
        P(("ens", "gx", "gy")),
    )
    return jax.shard_map(
        body,
        mesh=mesh,
        in_specs=placed,
        out_specs=(P("ens", None, "gx", "gy"), P("ens", None, "gx", "gy")),
        check_vma=False,
    )
```

```python
import functools

import jax
import jax.numpy as jnp
from jax import lax
from jax.experimental import pallas as pl
from jax.experimental.pallas import tpu as pltpu
from jax.sharding import PartitionSpec as P

WIN = 128
CAP = 2
ROWS = 4
LANES = 128
SUB = 8

time_step = 0.1
diffusion = 0.2
VMEM_LIMIT = 32 * 1024 * 1024


def held(array):
    return pltpu.with_memory_space_constraint(array, pltpu.VMEM)


def left(array):
    return pltpu.with_memory_space_constraint(array, pltpu.HBM)


def lane_of(shape):
    return lax.broadcasted_iota(jnp.int32, shape, len(shape) - 1)


def row_of(shape):
    return lax.broadcasted_iota(jnp.int32, shape, len(shape) - 2)


def send_blocks(pick, count, weights_ref, dest_ref, window_ref, picked_ref, counts_ref, out_ref):
    blocks = weights_ref.shape[0]
    out_ref[...] = jnp.zeros_like(out_ref)

    def clear(d, carry):
        counts_ref[d] = 0
        return carry

    lax.fori_loop(0, out_ref.shape[0], clear, 0)
    picked_ref[...] = jnp.zeros_like(picked_ref)
    for k in range(blocks):
        for f in range(count):
            picked_ref[k, pl.ds(f, 1), :] = pick(k, f)
    row = row_of((SUB, LANES))
    lane = lane_of((SUB, LANES))
    for k in range(blocks):
        values = picked_ref[k]
        high = values.astype(jnp.bfloat16)
        low = (values - high.astype(jnp.float32)).astype(jnp.bfloat16)
        left = jnp.concatenate([high.astype(jnp.float32), low.astype(jnp.float32)], axis=0).astype(jnp.bfloat16)
        weight = weights_ref[k]
        weight_high = weight.astype(jnp.bfloat16)
        weight_low = (weight - weight_high.astype(jnp.float32)).astype(jnp.bfloat16)
        right = jnp.concatenate([weight_high, weight_low], axis=0)
        product = lax.dot_general(left, right, (((1,), (1,)), ((), ())), preferred_element_type=jnp.float32)
        total = product[:SUB, :WIN] + (product[SUB:, :WIN] + product[:SUB, WIN:])
        d = dest_ref[k]
        slot = counts_ref[d]
        counts_ref[d] = slot + 1
        onehot = jnp.where(lane == window_ref[k], 1.0, 0.0)
        total = jnp.where(row == ROWS - 1, onehot, jnp.where(row < count, total, 0.0))
        total = jnp.where(slot == 0, total, jnp.concatenate([total[ROWS:], total[:ROWS]], axis=0))
        out_ref[d] = out_ref[d] + total


def receive_blocks(arrived_ref, count):
    slots = arrived_ref.shape[0] // ROWS
    onehot = arrived_ref[pl.ds(ROWS - 1, slots, stride=ROWS), :]
    fields = [arrived_ref[pl.ds(f, slots, stride=ROWS), :] for f in range(count)]
    return [
        lax.dot_general(
            onehot, field, (((0,), (0,)), ((), ())), precision=lax.Precision.HIGHEST, preferred_element_type=jnp.float32
        )
        for field in fields
    ]


def sea_send_kernel(
    dest_ref, source_ref, window_ref, ocean_ref, weights_ref, out_ref, picked_ref, counts_ref, surface_ref
):
    rows, cols = ocean_ref.shape[2:]
    halves = cols // WIN
    for f in range(3):
        for h in range(halves):
            surface_ref[f, pl.ds(h, rows, stride=halves), :] = ocean_ref[(0, 2, 3)[f], 0, :, pl.ds(h * WIN, WIN)]

    def pick(k, f):
        return surface_ref[f, pl.ds(source_ref[k], 1), :]

    send_blocks(pick, 3, weights_ref, dest_ref, window_ref, picked_ref, counts_ref, out_ref)


def sea_send(tiles, ocean, weights, dest, source, window):
    blocks = weights.shape[0]
    smem = pl.BlockSpec(memory_space=pltpu.SMEM)
    return pl.pallas_call(
        sea_send_kernel,
        grid=(1,),
        out_shape=jax.ShapeDtypeStruct((tiles, CAP * ROWS, WIN), jnp.float32),
        in_specs=[
            smem,
            smem,
            smem,
            pl.BlockSpec((4, 1) + ocean.shape[2:], lambda i: (0, 0, 0, 0)),
            pl.BlockSpec(weights.shape, lambda i: (0, 0, 0)),
        ],
        out_specs=pl.BlockSpec((tiles, CAP * ROWS, WIN), lambda i: (0, 0, 0)),
        scratch_shapes=[
            pltpu.VMEM((blocks, SUB, WIN), jnp.float32),
            pltpu.SMEM((tiles,), jnp.int32),
            pltpu.VMEM((3, ocean.shape[2] * ocean.shape[3] // WIN, WIN), jnp.float32),
        ],
        compiler_params=pltpu.CompilerParams(vmem_limit_bytes=VMEM_LIMIT),
        cost_estimate=pl.CostEstimate(flops=blocks * 2 * 16 * 128 * 256, bytes_accessed=2000000, transcendentals=0),
        name="sea_send",
    )(left(dest), left(source), left(window), left(ocean), left(weights))


def air_send_kernel(
    dest_ref, source_ref, window_ref, arrived_ref, atm_ref, weights_ref, out_ref, flux_ref, picked_ref, counts_ref
):
    rows = atm_ref.shape[2]
    on_air = [field[:rows] for field in receive_blocks(arrived_ref, 3)]
    relative_u = atm_ref[2, 0] - on_air[1]
    relative_v = atm_ref[3, 0] - on_air[2]
    wind_speed = jnp.sqrt(relative_u * relative_u + relative_v * relative_v + 1.0)
    flux_ref[0] = 0.5 * wind_speed * (on_air[0] - atm_ref[0, 0])
    flux_ref[1] = 0.4 * wind_speed * (0.8 * on_air[0] - atm_ref[1, 0])

    def pick(k, f):
        return flux_ref[f, pl.ds(source_ref[k], 1), :]

    send_blocks(pick, 2, weights_ref, dest_ref, window_ref, picked_ref, counts_ref, out_ref)


def air_send(arrived, atm, weights, dest, source, window):
    blocks = weights.shape[0]
    tiles = arrived.shape[0]
    rows, cols = atm.shape[2:]
    smem = pl.BlockSpec(memory_space=pltpu.SMEM)
    return pl.pallas_call(
        air_send_kernel,
        grid=(1,),
        out_shape=(
            jax.ShapeDtypeStruct((tiles, CAP * ROWS, WIN), jnp.float32),
            jax.ShapeDtypeStruct((2, rows, cols), jnp.float32),
        ),
        in_specs=[
            smem,
            smem,
            smem,
            pl.BlockSpec(memory_space=pltpu.VMEM),
            pl.BlockSpec((4, 1, rows, cols), lambda i: (0, 0, 0, 0)),
            pl.BlockSpec(memory_space=pltpu.VMEM),
        ],
        out_specs=(
            pl.BlockSpec((tiles, CAP * ROWS, WIN), lambda i: (0, 0, 0)),
            pl.BlockSpec((2, rows, cols), lambda i: (0, 0, 0)),
        ),
        scratch_shapes=[pltpu.VMEM((blocks, SUB, WIN), jnp.float32), pltpu.SMEM((tiles,), jnp.int32)],
        compiler_params=pltpu.CompilerParams(vmem_limit_bytes=VMEM_LIMIT),
        cost_estimate=pl.CostEstimate(flops=blocks * 2 * 16 * 128 * 256, bytes_accessed=2000000, transcendentals=0),
        name="air_send",
    )(left(dest), left(source), left(window), held(arrived.reshape(tiles * CAP * ROWS, WIN)), left(atm), held(weights))


def sea_forcing_kernel(arrived_ref, land_ref, before_ref, after_ref, summed_ref):
    rows, cols = land_ref.shape
    halves = cols // WIN
    for f, field in enumerate(receive_blocks(arrived_ref, 2)):
        summed_ref[f] = field
        for h in range(halves):
            span = pl.ds(h * WIN, WIN)
            forcing = summed_ref[f, pl.ds(h, rows, stride=halves), :] * (-0.5, 0.3)[f]
            change = jnp.where(land_ref[:, span] == 1, time_step * forcing, 0.0)
            after_ref[f, 0, :, span] = before_ref[f, 0, :, span] + change


def add_sea_forcing(arrived, land, sea_next):
    tiles = arrived.shape[0]
    rows, cols = land.shape
    return pl.pallas_call(
        sea_forcing_kernel,
        grid=(1,),
        out_shape=jax.ShapeDtypeStruct(sea_next.shape, jnp.float32),
        in_specs=[
            pl.BlockSpec(memory_space=pltpu.VMEM),
            pl.BlockSpec(memory_space=pltpu.VMEM),
            pl.BlockSpec((2, 1, rows, cols), lambda i: (0, 0, 0, 0)),
        ],
        out_specs=pl.BlockSpec((2, 1, rows, cols), lambda i: (0, 0, 0, 0)),
        scratch_shapes=[pltpu.VMEM((2, rows * cols // WIN, WIN), jnp.float32)],
        input_output_aliases={2: 0},
        compiler_params=pltpu.CompilerParams(vmem_limit_bytes=VMEM_LIMIT),
        cost_estimate=pl.CostEstimate(flops=4000000, bytes_accessed=600000, transcendentals=0),
        name="sea_forcing",
    )(held(arrived.reshape(tiles * CAP * ROWS, WIN)), held(land), sea_next)


def padded_levels(levels):
    return -(-levels // SUB) * SUB


CHUNKS = 2


def edges_kernel(gy_ref, atm_ref, ocean_ref, xlow_ref, xhigh_ref, y_ref, air, sea, sea_v, low, high, sems):
    air_levels, air_rows = atm_ref.shape[1:3]
    sea_levels, sea_rows, sea_cols = ocean_ref.shape[1:]
    halves = sea_cols // WIN
    pitch = padded_levels(air_levels)
    edge = jnp.where(gy_ref[0] == 0, LANES - 1, 0)
    span = pl.ds(pl.multiple_of(jnp.where(gy_ref[0] == 0, sea_cols - LANES, 0), LANES), LANES)

    def copies(chunk):
        a = pl.ds(chunk * (air_levels // CHUNKS), air_levels // CHUNKS)
        o = pl.ds(chunk * (sea_levels // CHUNKS), sea_levels // CHUNKS)
        pairs = [
            (atm_ref.at[:, a], air.at[:, a]),
            (ocean_ref.at[pl.ds(0, 2), o, :, span], sea.at[:, o]),
            (ocean_ref.at[3, o, :, span], sea_v.at[o]),
            (ocean_ref.at[pl.ds(0, 3), o, pl.ds(0, SUB)], low.at[:, o]),
            (ocean_ref.at[pl.ds(0, 3), o, pl.ds(sea_rows - SUB, SUB)], high.at[:, o]),
        ]
        return [pltpu.make_async_copy(src, dst, sems.at[chunk, i]) for i, (src, dst) in enumerate(pairs)]

    for chunk in range(CHUNKS):
        for copy in copies(chunk):
            copy.start()
    for f in range(3):
        for ref in (xlow_ref, xhigh_ref):
            ref[pl.ds((f + 1) * pitch - SUB, SUB), :] = jnp.zeros((SUB, LANES), jnp.float32)

    def put(total, column, to, lane):
        return jnp.where(lane == to, pltpu.roll(column, (to - edge + LANES) % LANES, 1), total)

    air_lane, sea_lane = lane_of((air_rows, LANES)), lane_of((sea_rows, LANES))
    tracers = v = jnp.zeros((air_rows, LANES), jnp.float32)
    total = jnp.zeros((sea_rows, LANES), jnp.float32)
    for chunk in range(CHUNKS):
        for copy in copies(chunk):
            copy.wait()
        for level in range(chunk * (air_levels // CHUNKS), (chunk + 1) * (air_levels // CHUNKS)):
            tracers = put(tracers, air[0, level], level, air_lane)
            tracers = put(tracers, air[1, level], LANES // 2 + level, air_lane)
            v = put(v, air[3, level], level, air_lane)
            for f in range(3):
                to = pl.ds(f * pitch + level, 1)
                xlow_ref[to, :] = air[f, level, pl.ds(0, 1), :]
                xhigh_ref[to, :] = air[f, level, pl.ds(air_rows - 1, 1), :]
        for level in range(chunk * (sea_levels // CHUNKS), (chunk + 1) * (sea_levels // CHUNKS)):
            total = put(total, sea[0, level], level, sea_lane)
            total = put(total, sea[1, level], sea_levels + level, sea_lane)
            total = put(total, sea_v[level], 2 * sea_levels + level, sea_lane)
            for f in range(3):
                for h in range(halves):
                    to = pl.ds(3 * pitch + (f * halves + h) * sea_levels + level, 1)
                    xlow_ref[to, :] = low[f, level, pl.ds(0, 1), pl.ds(h * WIN, WIN)]
                    xhigh_ref[to, :] = high[f, level, pl.ds(SUB - 1, 1), pl.ds(h * WIN, WIN)]
    y_ref[:air_rows] = tracers
    y_ref[air_rows : 2 * air_rows] = v
    y_ref[2 * air_rows :] = total


def edges(gy, atm, ocean):
    air_levels, air_rows, _ = atm.shape[1:]
    sea_levels, sea_rows, sea_cols = ocean.shape[1:]
    xrows = 3 * padded_levels(air_levels) + 3 * sea_levels * (sea_cols // WIN)
    yrows = 2 * air_rows + sea_rows
    x_shape = jax.ShapeDtypeStruct((xrows, LANES), jnp.float32)
    vmem = pl.BlockSpec(memory_space=pltpu.VMEM)
    hbm = pl.BlockSpec(memory_space=pl.ANY)
    return pl.pallas_call(
        edges_kernel,
        in_specs=[pl.BlockSpec(memory_space=pltpu.SMEM), hbm, hbm],
        out_specs=[vmem, vmem, vmem],
        out_shape=(x_shape, x_shape, jax.ShapeDtypeStruct((yrows, LANES), jnp.float32)),
        scratch_shapes=[
            pltpu.VMEM(atm.shape, jnp.float32),
            pltpu.VMEM((2, sea_levels, sea_rows, LANES), jnp.float32),
            pltpu.VMEM((sea_levels, sea_rows, LANES), jnp.float32),
            pltpu.VMEM((3, sea_levels, SUB, sea_cols), jnp.float32),
            pltpu.VMEM((3, sea_levels, SUB, sea_cols), jnp.float32),
            pltpu.SemaphoreType.DMA((CHUNKS, 5)),
        ],
        compiler_params=pltpu.CompilerParams(vmem_limit_bytes=VMEM_LIMIT),
        cost_estimate=pl.CostEstimate(flops=2000000, bytes_accessed=10000000, transcendentals=0),
        name="edges",
    )(gy, left(atm), left(ocean))


def step_level(fields, west, east, south, write):
    row = row_of((SUB, LANES))
    lane = lane_of((SUB, LANES))
    groups, halves = fields.groups, fields.halves
    first_row, last_row = row == 0, row == SUB - 1
    first_lane, last_lane = lane == 0, lane == LANES - 1

    def along_x(f, h, scale):
        tiles = [fields(f, r, h) for r in range(groups)]
        if scale is not None:
            tiles = [scale * t for t in tiles]
        down = [pltpu.roll(t, 1, 0) for t in tiles]
        up = [pltpu.roll(t, SUB - 1, 0) for t in tiles]
        before = [jnp.broadcast_to(west(f, h), (SUB, LANES))] + down[:-1]
        after = up[1:] + [jnp.broadcast_to(east(f, h), (SUB, LANES))]
        if scale is not None:
            before[0], after[-1] = scale * before[0], scale * after[-1]
        lows = [jnp.where(first_row, b, d) for b, d in zip(before, down)]
        highs = [jnp.where(last_row, a, u) for a, u in zip(after, up)]
        return tiles, lows, highs

    def along_y(f, r, tiles, scale):
        beyond = south(f, r)
        if scale is not None:
            beyond = scale * beyond
        right = [pltpu.roll(t, 1, 1) for t in tiles]
        left = [pltpu.roll(t, LANES - 1, 1) for t in tiles]
        lows = [jnp.where(first_lane, b, t) for b, t in zip([beyond] + right[:-1], right)]
        highs = [jnp.where(last_lane, b, t) for b, t in zip(left[1:] + [beyond], left)]
        return lows, highs

    scale = 0.25 * time_step
    mixing = time_step * diffusion
    moved = [[along_x(f, h, scale if f == 2 else None) for h in range(halves)] for f in range(3)]
    for r in range(groups):
        v = [scale * fields(3, r, h) for h in range(halves)]
        v_low, v_high = along_y(3, r, v, scale)
        sides = [along_y(f, r, [moved[f][h][0][r] for h in range(halves)], None) for f in range(2)]
        for h in range(halves):
            u, u_low, u_high = (part[r] for part in moved[2][h])
            centre = (1.0 - 4.0 * mixing) + ((u_low - u_high) + (v_low[h] - v_high[h]))
            x_high, x_low = (mixing - u) - u_high, (mixing + u) + u_low
            y_high, y_low = (mixing - v[h]) - v_high[h], (mixing + v[h]) + v_low[h]
            for f in range(2):
                q, q_low, q_high = (part[r] for part in moved[f][h])
                new = centre * q + (x_high * q_high + x_low * q_low)
                new = new + (y_high * sides[f][1][h] + y_low * sides[f][0][h])
                write(f, r, h, new, q)


class Fields:
    def __init__(self, ref, level):
        self.ref, self.level = ref, level
        self.groups, self.halves = ref.shape[2] // SUB, ref.shape[3] // LANES

    def __call__(self, f, r, h):
        return self.ref[f, self.level, pl.ds(r * SUB, SUB), pl.ds(h * LANES, LANES)]


STEPS = 5
AIR_UNROLL = 12
SEA_UNROLL = 8


def transport_kernel(gy_ref, atm_ref, ocean_ref, land_ref, flux_ref, xlow_ref, xhigh_ref, y_ref, air_ref, sea_ref):
    step = pl.program_id(0)
    air_levels, air_rows = atm_ref.shape[1:3]
    sea_levels, sea_rows, sea_cols = ocean_ref.shape[1:]
    all_air, all_sea = STEPS * air_levels, STEPS * sea_levels
    halves = sea_cols // LANES
    pitch = padded_levels(all_air)
    edge = jnp.where(gy_ref[0] == 0, LANES - 1, 0)
    at_edge = lane_of((SUB, LANES)) == edge

    def column(start, r, at):
        tile = y_ref[pl.ds(start + r * SUB, SUB), :]
        return jnp.where(at_edge, pltpu.roll(tile, (edge - at + LANES) % LANES, 1), 0.0)

    def air_level(level):
        here = step * air_levels + level

        def beyond(f, r):
            start = air_rows if f == 3 else 0
            return column(start, r, (LANES // 2 if f == 1 else 0) + here)

        stores = []

        def write(f, r, h, new, q):
            stores.append((f, level, pl.ds(r * SUB, SUB), new))

        step_level(
            Fields(atm_ref, level),
            lambda f, h: xlow_ref[pl.ds(f * pitch + here, 1), :],
            lambda f, h: xhigh_ref[pl.ds(f * pitch + here, 1), :],
            beyond,
            write,
        )
        return stores

    def some_air(i, carry):
        stores = []
        for level in range(AIR_UNROLL):
            stores += air_level(i * AIR_UNROLL + level)
        for *place, new in stores:
            air_ref[tuple(place)] = new
        return carry

    lax.fori_loop(0, air_levels // AIR_UNROLL, some_air, 0)

    @pl.when(step == 0)
    def _():
        for f in range(2):
            air_ref[f, 0] = air_ref[f, 0] + time_step * flux_ref[f]

    def sea_level(level):
        here = step * sea_levels + level

        def beyond(f, r):
            return column(2 * air_rows, r, (2 if f == 3 else f) * all_sea + here)

        stores = []

        def write(f, r, h, new, q):
            rows, span = pl.ds(r * SUB, SUB), pl.ds(h * LANES, LANES)
            stores.append((f, level, rows, span, jnp.where(land_ref[rows, span] == 1, new, q)))

        step_level(
            Fields(ocean_ref, level),
            lambda f, h: xlow_ref[pl.ds(3 * pitch + (f * halves + h) * all_sea + here, 1), :],
            lambda f, h: xhigh_ref[pl.ds(3 * pitch + (f * halves + h) * all_sea + here, 1), :],
            beyond,
            write,
        )
        return stores

    def some_sea(i, carry):
        stores = []
        for level in range(SEA_UNROLL):
            stores += sea_level(i * SEA_UNROLL + level)
        for *place, new in stores:
            sea_ref[tuple(place)] = new
        return carry

    lax.fori_loop(0, sea_levels // SEA_UNROLL, some_sea, 0)


def transport(gy, atm, ocean, land, flux, xlow, xhigh, y):
    air_levels, air_rows, _ = atm.shape[1:]
    sea_levels, sea_rows, sea_cols = ocean.shape[1:]
    a, o = air_levels // STEPS, sea_levels // STEPS
    vmem = pl.BlockSpec(memory_space=pltpu.VMEM)
    return pl.pallas_call(
        transport_kernel,
        grid=(STEPS,),
        in_specs=[
            pl.BlockSpec(memory_space=pltpu.SMEM),
            pl.BlockSpec((4, a, air_rows, LANES), lambda i: (0, i, 0, 0)),
            pl.BlockSpec((4, o, sea_rows, sea_cols), lambda i: (0, i, 0, 0)),
        ]
        + [vmem] * 5,
        out_specs=[
            pl.BlockSpec((2, a, air_rows, LANES), lambda i: (0, i, 0, 0)),
            pl.BlockSpec((2, o, sea_rows, sea_cols), lambda i: (0, i, 0, 0)),
        ],
        out_shape=(
            jax.ShapeDtypeStruct((2,) + atm.shape[1:], jnp.float32),
            jax.ShapeDtypeStruct((2,) + ocean.shape[1:], jnp.float32),
        ),
        compiler_params=pltpu.CompilerParams(vmem_limit_bytes=VMEM_LIMIT),
        cost_estimate=pl.CostEstimate(flops=60000000, bytes_accessed=22000000, transcendentals=0),
        name="transport",
    )(gy, left(atm), left(ocean), held(land), held(flux), held(xlow), held(xhigh), held(y))


def body(
    atm_fields,
    ocean_fields,
    land_sea,
    sea_weights,
    sea_dest,
    sea_source,
    sea_window,
    air_weights,
    air_dest,
    air_source,
    air_window,
):
    width_x, width_y = lax.axis_size("gx"), lax.axis_size("gy")
    assert width_y == 2
    tiles = width_x * width_y
    gy = lax.axis_index("gy").astype(jnp.int32).reshape(1)
    exchange = functools.partial(lax.all_to_all, axis_name=("gx", "gy"), split_axis=0, concat_axis=0, tiled=True)
    forward = [(i, i + 1) for i in range(width_x - 1)]
    backward = [(i + 1, i) for i in range(width_x - 1)]

    to_air = sea_send(tiles, ocean_fields, sea_weights, sea_dest.reshape(-1), sea_source, sea_window)
    on_air = exchange(to_air)
    low, high, side = edges(gy, atm_fields, ocean_fields)
    side = lax.ppermute(side, "gy", [(0, 1), (1, 0)])
    xlow = lax.ppermute(high, "gx", forward)
    xhigh = lax.ppermute(low, "gx", backward)
    on_air, side = lax.optimization_barrier((on_air, side))
    to_sea, fluxes = air_send(on_air, atm_fields, air_weights, air_dest.reshape(-1), air_source, air_window)
    on_sea = exchange(to_sea)
    air_next, sea_next = transport(gy, atm_fields, ocean_fields, land_sea, fluxes, xlow, xhigh, side)
    sea_next = add_sea_forcing(on_sea, land_sea, sea_next)
    return (air_next, sea_next)


def solution(mesh):
    placed = (
        P("ens", None, "gx", "gy"),
        P("ens", None, "gx", "gy"),
        P(("ens", "gx"), "gy"),
        P(("ens", "gx", "gy"), None, None),
        P(("ens", "gx", "gy"), None),
        P(("ens", "gx", "gy")),
        P(("ens", "gx", "gy")),
        P(("ens", "gx", "gy"), None, None),
        P(("ens", "gx", "gy"), None),
        P(("ens", "gx", "gy")),
        P(("ens", "gx", "gy")),
    )
    return jax.shard_map(
        body,
        mesh=mesh,
        in_specs=placed,
        out_specs=(P("ens", None, "gx", "gy"), P("ens", None, "gx", "gy")),
        check_vma=False,
    )
```

```python
import functools

import jax
import jax.numpy as jnp
from jax import lax
from jax.experimental import pallas as pl
from jax.experimental.pallas import tpu as pltpu
from jax.sharding import PartitionSpec as P

WIN = 128
CAP = 2
ROWS = 4
LANES = 128
SUB = 8

time_step = 0.1
diffusion = 0.2
VMEM_LIMIT = 40 * 1024 * 1024


def held(array):
    return pltpu.with_memory_space_constraint(array, pltpu.VMEM)


def left(array):
    return pltpu.with_memory_space_constraint(array, pltpu.HBM)


def lane_of(shape):
    return lax.broadcasted_iota(jnp.int32, shape, len(shape) - 1)


def row_of(shape):
    return lax.broadcasted_iota(jnp.int32, shape, len(shape) - 2)


def send_blocks(pick, count, weights_ref, dest_ref, window_ref, picked_ref, counts_ref, out_ref):
    blocks = weights_ref.shape[0]
    out_ref[...] = jnp.zeros_like(out_ref)

    def clear(d, carry):
        counts_ref[d] = 0
        return carry

    lax.fori_loop(0, out_ref.shape[0], clear, 0)
    picked_ref[...] = jnp.zeros_like(picked_ref)
    for k in range(blocks):
        for f in range(count):
            picked_ref[k, pl.ds(f, 1), :] = pick(k, f)
    row = row_of((SUB, LANES))
    lane = lane_of((SUB, LANES))
    for k in range(blocks):
        values = picked_ref[k]
        high = values.astype(jnp.bfloat16)
        low = (values - high.astype(jnp.float32)).astype(jnp.bfloat16)
        left = jnp.concatenate([high.astype(jnp.float32), low.astype(jnp.float32)], axis=0).astype(jnp.bfloat16)
        weight = weights_ref[k]
        weight_high = weight.astype(jnp.bfloat16)
        weight_low = (weight - weight_high.astype(jnp.float32)).astype(jnp.bfloat16)
        right = jnp.concatenate([weight_high, weight_low], axis=0)
        product = lax.dot_general(left, right, (((1,), (1,)), ((), ())), preferred_element_type=jnp.float32)
        total = product[:SUB, :WIN] + (product[SUB:, :WIN] + product[:SUB, WIN:])
        d = dest_ref[k]
        slot = counts_ref[d]
        counts_ref[d] = slot + 1
        onehot = jnp.where(lane == window_ref[k], 1.0, 0.0)
        total = jnp.where(row == ROWS - 1, onehot, jnp.where(row < count, total, 0.0))
        total = jnp.where(slot == 0, total, jnp.concatenate([total[ROWS:], total[:ROWS]], axis=0))
        out_ref[d] = out_ref[d] + total


def receive_blocks(arrived_ref, count):
    slots = arrived_ref.shape[0] // ROWS
    onehot = arrived_ref[pl.ds(ROWS - 1, slots, stride=ROWS), :]
    fields = [arrived_ref[pl.ds(f, slots, stride=ROWS), :] for f in range(count)]
    return [
        lax.dot_general(
            onehot, field, (((0,), (0,)), ((), ())), precision=lax.Precision.HIGHEST, preferred_element_type=jnp.float32
        )
        for field in fields
    ]


def sea_send_kernel(
    dest_ref, source_ref, window_ref, ocean_ref, weights_ref, out_ref, picked_ref, counts_ref, surface_ref
):
    rows, cols = ocean_ref.shape[2:]
    halves = cols // WIN
    for f in range(3):
        for h in range(halves):
            surface_ref[f, pl.ds(h, rows, stride=halves), :] = ocean_ref[(0, 2, 3)[f], 0, :, pl.ds(h * WIN, WIN)]

    def pick(k, f):
        return surface_ref[f, pl.ds(source_ref[k], 1), :]

    send_blocks(pick, 3, weights_ref, dest_ref, window_ref, picked_ref, counts_ref, out_ref)


def sea_send(tiles, ocean, weights, dest, source, window):
    blocks = weights.shape[0]
    smem = pl.BlockSpec(memory_space=pltpu.SMEM)
    return pl.pallas_call(
        sea_send_kernel,
        grid=(1,),
        out_shape=jax.ShapeDtypeStruct((tiles, CAP * ROWS, WIN), jnp.float32),
        in_specs=[
            smem,
            smem,
            smem,
            pl.BlockSpec((4, 1) + ocean.shape[2:], lambda i: (0, 0, 0, 0)),
            pl.BlockSpec(weights.shape, lambda i: (0, 0, 0)),
        ],
        out_specs=pl.BlockSpec((tiles, CAP * ROWS, WIN), lambda i: (0, 0, 0)),
        scratch_shapes=[
            pltpu.VMEM((blocks, SUB, WIN), jnp.float32),
            pltpu.SMEM((tiles,), jnp.int32),
            pltpu.VMEM((3, ocean.shape[2] * ocean.shape[3] // WIN, WIN), jnp.float32),
        ],
        compiler_params=pltpu.CompilerParams(vmem_limit_bytes=VMEM_LIMIT),
        cost_estimate=pl.CostEstimate(flops=blocks * 2 * 16 * 128 * 256, bytes_accessed=2000000, transcendentals=0),
        name="sea_send",
    )(left(dest), left(source), left(window), left(ocean), left(weights))


def air_send_kernel(
    dest_ref, source_ref, window_ref, arrived_ref, atm_ref, weights_ref, out_ref, flux_ref, picked_ref, counts_ref
):
    rows = atm_ref.shape[2]
    on_air = [field[:rows] for field in receive_blocks(arrived_ref, 3)]
    relative_u = atm_ref[2, 0] - on_air[1]
    relative_v = atm_ref[3, 0] - on_air[2]
    wind_speed = jnp.sqrt(relative_u * relative_u + relative_v * relative_v + 1.0)
    flux_ref[0] = 0.5 * wind_speed * (on_air[0] - atm_ref[0, 0])
    flux_ref[1] = 0.4 * wind_speed * (0.8 * on_air[0] - atm_ref[1, 0])

    def pick(k, f):
        return flux_ref[f, pl.ds(source_ref[k], 1), :]

    send_blocks(pick, 2, weights_ref, dest_ref, window_ref, picked_ref, counts_ref, out_ref)


def air_send(arrived, atm, weights, dest, source, window):
    blocks = weights.shape[0]
    tiles = arrived.shape[0]
    rows, cols = atm.shape[2:]
    smem = pl.BlockSpec(memory_space=pltpu.SMEM)
    return pl.pallas_call(
        air_send_kernel,
        grid=(1,),
        out_shape=(
            jax.ShapeDtypeStruct((tiles, CAP * ROWS, WIN), jnp.float32),
            jax.ShapeDtypeStruct((2, rows, cols), jnp.float32),
        ),
        in_specs=[
            smem,
            smem,
            smem,
            pl.BlockSpec(memory_space=pltpu.VMEM),
            pl.BlockSpec((4, 1, rows, cols), lambda i: (0, 0, 0, 0)),
            pl.BlockSpec(memory_space=pltpu.VMEM),
        ],
        out_specs=(
            pl.BlockSpec((tiles, CAP * ROWS, WIN), lambda i: (0, 0, 0)),
            pl.BlockSpec((2, rows, cols), lambda i: (0, 0, 0)),
        ),
        scratch_shapes=[pltpu.VMEM((blocks, SUB, WIN), jnp.float32), pltpu.SMEM((tiles,), jnp.int32)],
        compiler_params=pltpu.CompilerParams(vmem_limit_bytes=VMEM_LIMIT),
        cost_estimate=pl.CostEstimate(flops=blocks * 2 * 16 * 128 * 256, bytes_accessed=2000000, transcendentals=0),
        name="air_send",
    )(left(dest), left(source), left(window), held(arrived.reshape(tiles * CAP * ROWS, WIN)), left(atm), held(weights))


def sea_forcing_kernel(arrived_ref, land_ref, before_ref, after_ref, summed_ref):
    rows, cols = land_ref.shape
    halves = cols // WIN
    for f, field in enumerate(receive_blocks(arrived_ref, 2)):
        summed_ref[f] = field
        for h in range(halves):
            span = pl.ds(h * WIN, WIN)
            forcing = summed_ref[f, pl.ds(h, rows, stride=halves), :] * (-0.5, 0.3)[f]
            change = jnp.where(land_ref[:, span] == 1, time_step * forcing, 0.0)
            after_ref[f, 0, :, span] = before_ref[f, 0, :, span] + change


def add_sea_forcing(arrived, land, sea_next):
    tiles = arrived.shape[0]
    rows, cols = land.shape
    return pl.pallas_call(
        sea_forcing_kernel,
        grid=(1,),
        out_shape=jax.ShapeDtypeStruct(sea_next.shape, jnp.float32),
        in_specs=[
            pl.BlockSpec(memory_space=pltpu.VMEM),
            pl.BlockSpec(memory_space=pltpu.VMEM),
            pl.BlockSpec((2, 1, rows, cols), lambda i: (0, 0, 0, 0)),
        ],
        out_specs=pl.BlockSpec((2, 1, rows, cols), lambda i: (0, 0, 0, 0)),
        scratch_shapes=[pltpu.VMEM((2, rows * cols // WIN, WIN), jnp.float32)],
        input_output_aliases={2: 0},
        compiler_params=pltpu.CompilerParams(vmem_limit_bytes=VMEM_LIMIT),
        cost_estimate=pl.CostEstimate(flops=4000000, bytes_accessed=600000, transcendentals=0),
        name="sea_forcing",
    )(held(arrived.reshape(tiles * CAP * ROWS, WIN)), held(land), sea_next)


def padded_levels(levels):
    return -(-levels // SUB) * SUB


CHUNKS = 2


def edges_kernel(gy_ref, atm_ref, ocean_ref, xlow_ref, xhigh_ref, y_ref, air, sea, sea_v, low, high, sems):
    air_levels, air_rows = atm_ref.shape[1:3]
    sea_levels, sea_rows, sea_cols = ocean_ref.shape[1:]
    halves = sea_cols // WIN
    pitch = padded_levels(air_levels)
    edge = jnp.where(gy_ref[0] == 0, LANES - 1, 0)
    span = pl.ds(pl.multiple_of(jnp.where(gy_ref[0] == 0, sea_cols - LANES, 0), LANES), LANES)

    def copies(chunk):
        a = pl.ds(chunk * (air_levels // CHUNKS), air_levels // CHUNKS)
        o = pl.ds(chunk * (sea_levels // CHUNKS), sea_levels // CHUNKS)
        pairs = [
            (atm_ref.at[:, a], air.at[:, a]),
            (ocean_ref.at[pl.ds(0, 2), o, :, span], sea.at[:, o]),
            (ocean_ref.at[3, o, :, span], sea_v.at[o]),
            (ocean_ref.at[pl.ds(0, 3), o, pl.ds(0, SUB)], low.at[:, o]),
            (ocean_ref.at[pl.ds(0, 3), o, pl.ds(sea_rows - SUB, SUB)], high.at[:, o]),
        ]
        return [pltpu.make_async_copy(src, dst, sems.at[chunk, i]) for i, (src, dst) in enumerate(pairs)]

    for chunk in range(CHUNKS):
        for copy in copies(chunk):
            copy.start()
    for f in range(3):
        for ref in (xlow_ref, xhigh_ref):
            ref[pl.ds((f + 1) * pitch - SUB, SUB), :] = jnp.zeros((SUB, LANES), jnp.float32)

    def put(total, column, to, lane):
        return jnp.where(lane == to, pltpu.roll(column, (to - edge + LANES) % LANES, 1), total)

    air_lane, sea_lane = lane_of((air_rows, LANES)), lane_of((sea_rows, LANES))
    tracers = v = jnp.zeros((air_rows, LANES), jnp.float32)
    total = jnp.zeros((sea_rows, LANES), jnp.float32)
    for chunk in range(CHUNKS):
        for copy in copies(chunk):
            copy.wait()
        for level in range(chunk * (air_levels // CHUNKS), (chunk + 1) * (air_levels // CHUNKS)):
            tracers = put(tracers, air[0, level], level, air_lane)
            tracers = put(tracers, air[1, level], LANES // 2 + level, air_lane)
            v = put(v, air[3, level], level, air_lane)
            for f in range(3):
                to = pl.ds(f * pitch + level, 1)
                xlow_ref[to, :] = air[f, level, pl.ds(0, 1), :]
                xhigh_ref[to, :] = air[f, level, pl.ds(air_rows - 1, 1), :]
        for level in range(chunk * (sea_levels // CHUNKS), (chunk + 1) * (sea_levels // CHUNKS)):
            total = put(total, sea[0, level], level, sea_lane)
            total = put(total, sea[1, level], sea_levels + level, sea_lane)
            total = put(total, sea_v[level], 2 * sea_levels + level, sea_lane)
            for f in range(3):
                for h in range(halves):
                    to = pl.ds(3 * pitch + (f * halves + h) * sea_levels + level, 1)
                    xlow_ref[to, :] = low[f, level, pl.ds(0, 1), pl.ds(h * WIN, WIN)]
                    xhigh_ref[to, :] = high[f, level, pl.ds(SUB - 1, 1), pl.ds(h * WIN, WIN)]
    y_ref[:air_rows] = tracers
    y_ref[air_rows : 2 * air_rows] = v
    y_ref[2 * air_rows :] = total


def edges(gy, atm, ocean):
    air_levels, air_rows, _ = atm.shape[1:]
    sea_levels, sea_rows, sea_cols = ocean.shape[1:]
    xrows = 3 * padded_levels(air_levels) + 3 * sea_levels * (sea_cols // WIN)
    yrows = 2 * air_rows + sea_rows
    x_shape = jax.ShapeDtypeStruct((xrows, LANES), jnp.float32)
    vmem = pl.BlockSpec(memory_space=pltpu.VMEM)
    hbm = pl.BlockSpec(memory_space=pl.ANY)
    return pl.pallas_call(
        edges_kernel,
        in_specs=[pl.BlockSpec(memory_space=pltpu.SMEM), hbm, hbm],
        out_specs=[vmem, vmem, vmem],
        out_shape=(x_shape, x_shape, jax.ShapeDtypeStruct((yrows, LANES), jnp.float32)),
        scratch_shapes=[
            pltpu.VMEM(atm.shape, jnp.float32),
            pltpu.VMEM((2, sea_levels, sea_rows, LANES), jnp.float32),
            pltpu.VMEM((sea_levels, sea_rows, LANES), jnp.float32),
            pltpu.VMEM((3, sea_levels, SUB, sea_cols), jnp.float32),
            pltpu.VMEM((3, sea_levels, SUB, sea_cols), jnp.float32),
            pltpu.SemaphoreType.DMA((CHUNKS, 5)),
        ],
        compiler_params=pltpu.CompilerParams(vmem_limit_bytes=VMEM_LIMIT),
        cost_estimate=pl.CostEstimate(flops=2000000, bytes_accessed=10000000, transcendentals=0),
        name="edges",
    )(gy, left(atm), left(ocean))


STEPS = 5
PAD = 8


def beyond_columns(gy, mine, v_mine, other, v_other):
    scale, mixing = 0.25 * time_step, time_step * diffusion
    sign = jnp.where(gy == 0, -scale, scale)
    return mixing * other + sign * ((v_mine + v_other) * other + v_other * mine)


def step_level(ref, index, groups, halves, beyond, write):
    lane = lane_of((SUB, LANES))
    first_lane, last_lane = lane == 0, lane == LANES - 1
    scale, mixing = 0.25 * time_step, time_step * diffusion

    def rows(f, h, r, offset):
        return ref[index(f, h) + (pl.ds(PAD + r * SUB + offset, SUB), slice(None))]

    def along_y(tiles):
        right = [pltpu.roll(t, 1, 1) for t in tiles]
        left = [pltpu.roll(t, LANES - 1, 1) for t in tiles]
        lows = [jnp.where(first_lane, b, t) for b, t in zip([0.0] + right[:-1], right)]
        highs = [jnp.where(last_lane, b, t) for b, t in zip(left[1:] + [0.0], left)]
        return lows, highs

    for r in range(groups):
        q = [[rows(f, h, r, 0) for h in range(halves)] for f in range(2)]
        v = [scale * rows(3, h, r, 0) for h in range(halves)]
        v_low, v_high = along_y(v)
        sides = [along_y(q[f]) for f in range(2)]
        for h in range(halves):
            u, u_low, u_high = (scale * rows(2, h, r, offset) for offset in (0, -1, 1))
            centre = (1.0 - 4.0 * mixing) + ((u_low - u_high) + (v_low[h] - v_high[h]))
            x_high, x_low = (mixing - u) - u_high, (mixing + u) + u_low
            y_high, y_low = (mixing - v[h]) - v_high[h], (mixing + v[h]) + v_low[h]
            for f in range(2):
                new = centre * q[f][h] + (x_high * rows(f, h, r, 1) + x_low * rows(f, h, r, -1))
                new = new + (y_high * sides[f][1][h] + y_low * sides[f][0][h])
                write(f, r, h, new + beyond(f, r, h), q[f][h])


def transport_kernel(
    gy_ref,
    atm_ref,
    ocean_ref,
    land_ref,
    flux_ref,
    xlow_ref,
    xhigh_ref,
    mine_ref,
    y_ref,
    air_ref,
    sea_ref,
    air,
    sea,
    air_new,
    sea_new,
    air_edge,
    sea_edge,
    in_sems,
    out_sems,
):
    all_air, air_rows = atm_ref.shape[1:3]
    all_sea, sea_rows, sea_cols = ocean_ref.shape[1:]
    a, o = all_air // STEPS, all_sea // STEPS
    halves = sea_cols // LANES
    pitch = padded_levels(all_air)
    gy = gy_ref[0]

    def air_in(step):
        levels = pl.ds(step * a, a)
        yield pltpu.make_async_copy(
            atm_ref.at[:, levels], air.at[:, levels, pl.ds(PAD, air_rows)], in_sems.at[step, halves]
        )

    def sea_in(step):
        levels = pl.ds(step * o, o)
        for h in range(halves):
            yield pltpu.make_async_copy(
                ocean_ref.at[:, levels, :, pl.ds(h * LANES, LANES)],
                sea.at[h, :, levels, pl.ds(PAD, sea_rows)],
                in_sems.at[step, h],
            )

    def air_out(step):
        levels = pl.ds(step * a, a)
        return pltpu.make_async_copy(air_new.at[:, levels], air_ref.at[:, levels], out_sems.at[step, 0])

    def sea_out(step):
        levels = pl.ds(step * o, o)
        return pltpu.make_async_copy(sea_new.at[:, levels], sea_ref.at[:, levels], out_sems.at[step, 1])

    for step in range(STEPS):
        for copy in (*air_in(step), *sea_in(step)):
            copy.start()

    lane = lane_of((air_rows, LANES))
    mine, other = mine_ref[:air_rows], y_ref[:air_rows]

    def twice(v):
        return jnp.where(lane < LANES // 2, v, pltpu.roll(v, LANES // 2, 1))

    v_mine, v_other = twice(mine_ref[air_rows : 2 * air_rows]), twice(y_ref[air_rows : 2 * air_rows])
    air_edge[...] = beyond_columns(gy, mine, v_mine, other, v_other)
    lane = lane_of((sea_rows, LANES))
    mine, other = mine_ref[2 * air_rows :], y_ref[2 * air_rows :]

    def both(columns):
        first, second = (pltpu.roll(columns, LANES - n * all_sea, 1) for n in (2, 1))
        return jnp.where(lane < all_sea, first, second)

    sea_edge[...] = beyond_columns(gy, mine, both(mine), other, both(other))

    edge = jnp.where(gy == 0, LANES - 1, 0)
    lane = lane_of((SUB, LANES))
    at_first, at_last = (lane == 0) & (gy != 0), (lane == LANES - 1) & (gy == 0)
    at_edge = lane == edge

    def column(ref, r, at):
        return pltpu.roll(ref[pl.ds(r * SUB, SUB), :], (edge - at + LANES) % LANES, 1)

    def some_levels(step, carry):
        for copy in air_in(step):
            copy.wait()
        for j in range(a):
            level = step * a + j
            for f in range(3):
                air[f, level, pl.ds(PAD - 1, 1), :] = xlow_ref[pl.ds(f * pitch + level, 1), :]
                air[f, level, pl.ds(PAD + air_rows, 1), :] = xhigh_ref[pl.ds(f * pitch + level, 1), :]
        stores = []
        for j in range(a):
            level = step * a + j

            def beyond(f, r, h):
                return jnp.where(at_edge, column(air_edge, r, f * (LANES // 2) + level), 0.0)

            def write(f, r, h, new, q):
                stores.append((f, level, pl.ds(r * SUB, SUB), new))

            step_level(air, lambda f, h: (f, level), air_rows // SUB, 1, beyond, write)
        for *place, new in stores:
            air_new[tuple(place)] = new

        @pl.when(step == 0)
        def _():
            for f in range(2):
                air_new[f, 0] = air_new[f, 0] + time_step * flux_ref[f]

        air_out(step).start()
        for copy in sea_in(step):
            copy.wait()
        for j in range(o):
            level = step * o + j
            for f in range(3):
                for h in range(halves):
                    at = pl.ds(3 * pitch + (f * halves + h) * all_sea + level, 1)
                    sea[h, f, level, pl.ds(PAD - 1, 1), :] = xlow_ref[at, :]
                    sea[h, f, level, pl.ds(PAD + sea_rows, 1), :] = xhigh_ref[at, :]
        stores = []
        for j in range(o):
            level = step * o + j
            columns = {}

            def beyond(f, r, h):
                if (f, r) not in columns:
                    columns[f, r] = column(sea_edge, r, f * all_sea + level)
                added = columns[f, r]
                if h == 0:
                    return jnp.where(at_first, added, 0.0)
                return jnp.where(at_last, added, 0.0) if h == halves - 1 else 0.0

            def write(f, r, h, new, q):
                rows, span = pl.ds(r * SUB, SUB), pl.ds(h * LANES, LANES)
                stores.append((f, level, rows, span, jnp.where(land_ref[rows, span] == 1, new, q)))

            step_level(sea, lambda f, h: (h, f, level), sea_rows // SUB, halves, beyond, write)
        for *place, new in stores:
            sea_new[tuple(place)] = new
        sea_out(step).start()
        return carry

    lax.fori_loop(0, STEPS, some_levels, 0)
    for step in range(STEPS):
        air_out(step).wait()
        sea_out(step).wait()


def transport(gy, atm, ocean, land, flux, xlow, xhigh, mine, y):
    air_levels, air_rows, _ = atm.shape[1:]
    sea_levels, sea_rows, sea_cols = ocean.shape[1:]
    halves = sea_cols // LANES
    vmem = pl.BlockSpec(memory_space=pltpu.VMEM)
    hbm = pl.BlockSpec(memory_space=pltpu.HBM)
    air_shape, sea_shape = (2,) + atm.shape[1:], (2,) + ocean.shape[1:]
    return pl.pallas_call(
        transport_kernel,
        in_specs=[pl.BlockSpec(memory_space=pltpu.SMEM), hbm, hbm] + [vmem] * 6,
        out_specs=[hbm, hbm],
        out_shape=(jax.ShapeDtypeStruct(air_shape, jnp.float32), jax.ShapeDtypeStruct(sea_shape, jnp.float32)),
        scratch_shapes=[
            pltpu.VMEM((4, air_levels, air_rows + 2 * PAD, LANES), jnp.float32),
            pltpu.VMEM((halves, 4, sea_levels, sea_rows + 2 * PAD, LANES), jnp.float32),
            pltpu.VMEM(air_shape, jnp.float32),
            pltpu.VMEM(sea_shape, jnp.float32),
            pltpu.VMEM((air_rows, LANES), jnp.float32),
            pltpu.VMEM((sea_rows, LANES), jnp.float32),
            pltpu.SemaphoreType.DMA((STEPS, halves + 1)),
            pltpu.SemaphoreType.DMA((STEPS, 2)),
        ],
        compiler_params=pltpu.CompilerParams(vmem_limit_bytes=VMEM_LIMIT),
        cost_estimate=pl.CostEstimate(flops=60000000, bytes_accessed=22000000, transcendentals=0),
        name="transport",
    )(gy, left(atm), left(ocean), held(land), held(flux), held(xlow), held(xhigh), held(mine), held(y))


def body(
    atm_fields,
    ocean_fields,
    land_sea,
    sea_weights,
    sea_dest,
    sea_source,
    sea_window,
    air_weights,
    air_dest,
    air_source,
    air_window,
):
    width_x, width_y = lax.axis_size("gx"), lax.axis_size("gy")
    assert width_y == 2
    tiles = width_x * width_y
    gy = lax.axis_index("gy").astype(jnp.int32).reshape(1)
    exchange = functools.partial(lax.all_to_all, axis_name=("gx", "gy"), split_axis=0, concat_axis=0, tiled=True)
    forward = [(i, i + 1) for i in range(width_x - 1)]
    backward = [(i + 1, i) for i in range(width_x - 1)]

    to_air = sea_send(tiles, ocean_fields, sea_weights, sea_dest.reshape(-1), sea_source, sea_window)
    on_air = exchange(to_air)
    low, high, mine = edges(gy, atm_fields, ocean_fields)
    side = lax.ppermute(mine, "gy", [(0, 1), (1, 0)])
    xlow = lax.ppermute(high, "gx", forward)
    xhigh = lax.ppermute(low, "gx", backward)
    to_sea, fluxes = air_send(on_air, atm_fields, air_weights, air_dest.reshape(-1), air_source, air_window)
    to_sea, side = lax.optimization_barrier((to_sea, side))
    on_sea = exchange(to_sea)
    air_next, sea_next = transport(gy, atm_fields, ocean_fields, land_sea, fluxes, xlow, xhigh, mine, side)
    sea_next = add_sea_forcing(on_sea, land_sea, sea_next)
    return (air_next, sea_next)


def solution(mesh):
    placed = (
        P("ens", None, "gx", "gy"),
        P("ens", None, "gx", "gy"),
        P(("ens", "gx"), "gy"),
        P(("ens", "gx", "gy"), None, None),
        P(("ens", "gx", "gy"), None),
        P(("ens", "gx", "gy")),
        P(("ens", "gx", "gy")),
        P(("ens", "gx", "gy"), None, None),
        P(("ens", "gx", "gy"), None),
        P(("ens", "gx", "gy")),
        P(("ens", "gx", "gy")),
    )
    return jax.shard_map(
        body,
        mesh=mesh,
        in_specs=placed,
        out_specs=(P("ens", None, "gx", "gy"), P("ens", None, "gx", "gy")),
        check_vma=False,
    )
```

```python
import functools

import jax
import jax.numpy as jnp
from jax import lax
from jax.experimental import pallas as pl
from jax.experimental.pallas import tpu as pltpu
from jax.sharding import PartitionSpec as P

WIN = 128
CAP = 2
ROWS = 4
LANES = 128
SUB = 8

time_step = 0.1
diffusion = 0.2
VMEM_LIMIT = 40 * 1024 * 1024


def held(array):
    return pltpu.with_memory_space_constraint(array, pltpu.VMEM)


def left(array):
    return pltpu.with_memory_space_constraint(array, pltpu.HBM)


def lane_of(shape):
    return lax.broadcasted_iota(jnp.int32, shape, len(shape) - 1)


def row_of(shape):
    return lax.broadcasted_iota(jnp.int32, shape, len(shape) - 2)


def send_blocks(pick, count, weights_ref, dest_ref, window_ref, picked_ref, counts_ref, out_ref):
    blocks = weights_ref.shape[0]
    out_ref[...] = jnp.zeros_like(out_ref)

    def clear(d, carry):
        counts_ref[d] = 0
        return carry

    lax.fori_loop(0, out_ref.shape[0], clear, 0)
    picked_ref[...] = jnp.zeros_like(picked_ref)
    for k in range(blocks):
        for f in range(count):
            picked_ref[k, pl.ds(f, 1), :] = pick(k, f)
    row = row_of((SUB, LANES))
    lane = lane_of((SUB, LANES))
    for k in range(blocks):
        values = picked_ref[k]
        high = values.astype(jnp.bfloat16)
        low = (values - high.astype(jnp.float32)).astype(jnp.bfloat16)
        left = jnp.concatenate([high.astype(jnp.float32), low.astype(jnp.float32)], axis=0).astype(jnp.bfloat16)
        weight = weights_ref[k]
        weight_high = weight.astype(jnp.bfloat16)
        weight_low = (weight - weight_high.astype(jnp.float32)).astype(jnp.bfloat16)
        right = jnp.concatenate([weight_high, weight_low], axis=0)
        product = lax.dot_general(left, right, (((1,), (1,)), ((), ())), preferred_element_type=jnp.float32)
        total = product[:SUB, :WIN] + (product[SUB:, :WIN] + product[:SUB, WIN:])
        d = dest_ref[k]
        slot = counts_ref[d]
        counts_ref[d] = slot + 1
        onehot = jnp.where(lane == window_ref[k], 1.0, 0.0)
        total = jnp.where(row == ROWS - 1, onehot, jnp.where(row < count, total, 0.0))
        total = jnp.where(slot == 0, total, jnp.concatenate([total[ROWS:], total[:ROWS]], axis=0))
        out_ref[d] = out_ref[d] + total


def receive_blocks(arrived_ref, count):
    slots = arrived_ref.shape[0] // ROWS
    onehot = arrived_ref[pl.ds(ROWS - 1, slots, stride=ROWS), :]
    fields = [arrived_ref[pl.ds(f, slots, stride=ROWS), :] for f in range(count)]
    return [
        lax.dot_general(
            onehot, field, (((0,), (0,)), ((), ())), precision=lax.Precision.HIGHEST, preferred_element_type=jnp.float32
        )
        for field in fields
    ]


def index_copies(refs, held_refs, sems):
    return [pltpu.make_async_copy(src, dst, sems.at[i]) for i, (src, dst) in enumerate(zip(refs, held_refs))]


def air_send_kernel(
    dest_hbm,
    source_hbm,
    window_hbm,
    arrived_ref,
    some_air_ref,
    weights_ref,
    out_ref,
    flux_ref,
    picked_ref,
    counts_ref,
    dest_ref,
    source_ref,
    window_ref,
    sems,
):
    indices = index_copies((dest_hbm, source_hbm, window_hbm), (dest_ref, source_ref, window_ref), sems)
    for copy in indices:
        copy.start()
    rows = some_air_ref.shape[2]
    surface = [some_air_ref[f, 0] for f in range(4)]
    on_air = [field[:rows] for field in receive_blocks(arrived_ref, 3)]
    relative_u = surface[2] - on_air[1]
    relative_v = surface[3] - on_air[2]
    wind_speed = jnp.sqrt(relative_u * relative_u + relative_v * relative_v + 1.0)
    flux_ref[0] = 0.5 * wind_speed * (on_air[0] - surface[0])
    flux_ref[1] = 0.4 * wind_speed * (0.8 * on_air[0] - surface[1])

    for copy in indices:
        copy.wait()

    def pick(k, f):
        return flux_ref[f, pl.ds(source_ref[k], 1), :]

    send_blocks(pick, 2, weights_ref, dest_ref, window_ref, picked_ref, counts_ref, out_ref)


def air_send(arrived, some_air, weights, dest, source, window):
    blocks = weights.shape[0]
    tiles = arrived.shape[0]
    vmem = pl.BlockSpec(memory_space=pltpu.VMEM)
    hbm = pl.BlockSpec(memory_space=pltpu.HBM)
    return pl.pallas_call(
        air_send_kernel,
        in_specs=[hbm] * 3 + [vmem] * 3,
        out_specs=(vmem, vmem),
        out_shape=(
            pltpu.VMEM((tiles, CAP * ROWS, WIN), jnp.float32),
            pltpu.VMEM((2,) + some_air.shape[2:], jnp.float32),
        ),
        scratch_shapes=[pltpu.VMEM((blocks, SUB, WIN), jnp.float32), pltpu.SMEM((tiles,), jnp.int32)]
        + [pltpu.SMEM((blocks,), jnp.int32)] * 3
        + [pltpu.SemaphoreType.DMA((3,))],
        compiler_params=pltpu.CompilerParams(vmem_limit_bytes=VMEM_LIMIT),
        cost_estimate=pl.CostEstimate(flops=blocks * 2 * 16 * 128 * 256, bytes_accessed=2000000, transcendentals=0),
        name="air_send",
    )(
        left(dest),
        left(source),
        left(window),
        held(arrived.reshape(tiles * CAP * ROWS, WIN)),
        some_air,
        held(weights),
    )


def sea_forcing_kernel(arrived_ref, land_ref, top_ref, before_ref, after_ref, summed_ref, new_ref, sem):
    del before_ref
    rows, cols = land_ref.shape
    halves = cols // WIN
    for f, field in enumerate(receive_blocks(arrived_ref, 2)):
        summed_ref[f] = field
        for h in range(halves):
            span = pl.ds(h * WIN, WIN)
            forcing = summed_ref[f, pl.ds(h, rows, stride=halves), :] * (-0.5, 0.3)[f]
            change = jnp.where(land_ref[:, span] == 1, time_step * forcing, 0.0)
            new_ref[f, :, span] = top_ref[f, :, span] + change
    copy = pltpu.make_async_copy(new_ref, after_ref.at[:, 0], sem)
    copy.start()
    copy.wait()


def add_sea_forcing(arrived, land, top, sea_next):
    tiles = arrived.shape[0]
    rows, cols = land.shape
    vmem = pl.BlockSpec(memory_space=pltpu.VMEM)
    hbm = pl.BlockSpec(memory_space=pltpu.HBM)
    return pl.pallas_call(
        sea_forcing_kernel,
        in_specs=[vmem, vmem, vmem, hbm],
        out_specs=hbm,
        out_shape=jax.ShapeDtypeStruct(sea_next.shape, jnp.float32),
        scratch_shapes=[
            pltpu.VMEM((2, rows * cols // WIN, WIN), jnp.float32),
            pltpu.VMEM((2, rows, cols), jnp.float32),
            pltpu.SemaphoreType.DMA(()),
        ],
        input_output_aliases={3: 0},
        compiler_params=pltpu.CompilerParams(vmem_limit_bytes=VMEM_LIMIT),
        cost_estimate=pl.CostEstimate(flops=4000000, bytes_accessed=600000, transcendentals=0),
        name="sea_forcing",
    )(held(arrived.reshape(tiles * CAP * ROWS, WIN)), held(land), top, sea_next)


def padded_levels(levels):
    return -(-levels // SUB) * SUB


CHUNKS = 4


def first_kernel(
    dest_hbm,
    source_hbm,
    window_hbm,
    atm_ref,
    ocean_ref,
    weights_ref,
    out_ref,
    first_ref,
    second_ref,
    y_ref,
    some_air_ref,
    air,
    sea,
    sea_v,
    low,
    high,
    weights,
    top,
    windows,
    picked,
    counts,
    dest_ref,
    source_ref,
    window_ref,
    sems,
    weight_sems,
    top_sems,
    index_sems,
):
    air_levels, air_rows = atm_ref.shape[1:3]
    sea_levels, sea_rows, sea_cols = ocean_ref.shape[1:]
    halves = sea_cols // WIN
    pitch = padded_levels(air_levels)
    gx, gy, last_gx = lax.axis_index("gx"), lax.axis_index("gy"), lax.axis_size("gx") - 1
    even = gx % 2 == 0
    at_end = (gx == 0) | (gx == last_gx)
    edge = jnp.where(gy == 0, LANES - 1, 0)
    span = pl.ds(pl.multiple_of(jnp.where(gy == 0, sea_cols - LANES, 0), LANES), LANES)
    a, o = air_levels // CHUNKS, sea_levels // CHUNKS

    tops = [pltpu.make_async_copy(ocean_ref.at[f, 0], top.at[i], top_sems.at[i]) for i, f in enumerate((0, 2, 3))]
    weights_in = pltpu.make_async_copy(weights_ref, weights, weight_sems)

    def copies(chunk):
        air_span, sea_span = pl.ds(chunk * a, a), pl.ds(chunk * o, o)
        pairs = [
            (atm_ref.at[:, air_span], air.at[:, air_span]),
            (ocean_ref.at[pl.ds(0, 2), sea_span, :, span], sea.at[:, sea_span]),
            (ocean_ref.at[3, sea_span, :, span], sea_v.at[sea_span]),
            (ocean_ref.at[pl.ds(0, 3), sea_span, pl.ds(0, SUB)], low.at[:, sea_span]),
            (ocean_ref.at[pl.ds(0, 3), sea_span, pl.ds(sea_rows - SUB, SUB)], high.at[:, sea_span]),
        ]
        return [pltpu.make_async_copy(src, dst, sems.at[chunk, i]) for i, (src, dst) in enumerate(pairs)]

    indices = index_copies((dest_hbm, source_hbm, window_hbm), (dest_ref, source_ref, window_ref), index_sems)
    for copy in indices + tops:
        copy.start()
    weights_in.start()
    for chunk in range(CHUNKS):
        for copy in copies(chunk):
            copy.start()

    for copy in indices + tops:
        copy.wait()
    for f in range(3):
        for h in range(halves):
            windows[f, pl.ds(h, sea_rows, stride=halves), :] = top[f, :, pl.ds(h * WIN, WIN)]
    weights_in.wait()

    def pick(k, f):
        return windows[f, pl.ds(source_ref[k], 1), :]

    send_blocks(pick, 3, weights, dest_ref, window_ref, picked, counts, out_ref)

    for f in range(3):
        for ref in (first_ref, second_ref):
            ref[pl.ds((f + 1) * pitch - SUB, SUB), :] = jnp.zeros((SUB, LANES), jnp.float32)

    def put_rows(to, low_row, high_row):
        first_ref[pl.ds(to, 1), :] = jnp.where(even, high_row, low_row)
        second_ref[pl.ds(to, 1), :] = jnp.where(at_end, 0.0, jnp.where(even, low_row, high_row))

    def put(total, column, to, lane):
        return jnp.where(lane == to, pltpu.roll(column, (to - edge + LANES) % LANES, 1), total)

    air_lane, sea_lane = lane_of((air_rows, LANES)), lane_of((sea_rows, LANES))
    tracers = v = jnp.zeros((air_rows, LANES), jnp.float32)
    total = jnp.zeros((sea_rows, LANES), jnp.float32)
    for chunk in range(CHUNKS):
        for copy in copies(chunk):
            copy.wait()
        if chunk == 0:
            some_air_ref[...] = air[:, : some_air_ref.shape[1]]
        for level in range(chunk * a, (chunk + 1) * a):
            tracers = put(tracers, air[0, level], level, air_lane)
            tracers = put(tracers, air[1, level], LANES // 2 + level, air_lane)
            v = put(v, air[3, level], level, air_lane)
            for f in range(3):
                put_rows(f * pitch + level, air[f, level, pl.ds(0, 1), :], air[f, level, pl.ds(air_rows - 1, 1), :])
        for level in range(chunk * o, (chunk + 1) * o):
            total = put(total, sea[0, level], level, sea_lane)
            total = put(total, sea[1, level], sea_levels + level, sea_lane)
            total = put(total, sea_v[level], 2 * sea_levels + level, sea_lane)
            for f in range(3):
                for h in range(halves):
                    tile = pl.ds(h * WIN, WIN)
                    put_rows(
                        3 * pitch + (f * halves + h) * sea_levels + level,
                        low[f, level, pl.ds(0, 1), tile],
                        high[f, level, pl.ds(SUB - 1, 1), tile],
                    )
    y_ref[:air_rows] = tracers
    y_ref[air_rows : 2 * air_rows] = v
    y_ref[2 * air_rows :] = total


def first(tiles, atm, ocean, weights, dest, source, window):
    blocks = weights.shape[0]
    air_levels, air_rows, _ = atm.shape[1:]
    sea_levels, sea_rows, sea_cols = ocean.shape[1:]
    xrows = 3 * padded_levels(air_levels) + 3 * sea_levels * (sea_cols // WIN)
    yrows = 2 * air_rows + sea_rows
    vmem = pl.BlockSpec(memory_space=pltpu.VMEM)
    hbm = pl.BlockSpec(memory_space=pltpu.HBM)
    return pl.pallas_call(
        first_kernel,
        in_specs=[hbm] * 6,
        out_specs=[vmem] * 5,
        out_shape=(
            pltpu.VMEM((tiles, CAP * ROWS, WIN), jnp.float32),
            pltpu.VMEM((xrows, LANES), jnp.float32),
            pltpu.VMEM((xrows, LANES), jnp.float32),
            pltpu.VMEM((yrows, LANES), jnp.float32),
            pltpu.VMEM((4, air_levels // STEPS, air_rows, LANES), jnp.float32),
        ),
        scratch_shapes=[
            pltpu.VMEM(atm.shape, jnp.float32),
            pltpu.VMEM((2, sea_levels, sea_rows, LANES), jnp.float32),
            pltpu.VMEM((sea_levels, sea_rows, LANES), jnp.float32),
            pltpu.VMEM((3, sea_levels, SUB, sea_cols), jnp.float32),
            pltpu.VMEM((3, sea_levels, SUB, sea_cols), jnp.float32),
            pltpu.VMEM(weights.shape, jnp.float32),
            pltpu.VMEM((3, sea_rows, sea_cols), jnp.float32),
            pltpu.VMEM((3, sea_rows * sea_cols // WIN, WIN), jnp.float32),
            pltpu.VMEM((blocks, SUB, WIN), jnp.float32),
            pltpu.SMEM((tiles,), jnp.int32),
            pltpu.SMEM((blocks,), jnp.int32),
            pltpu.SMEM((blocks,), jnp.int32),
            pltpu.SMEM((blocks,), jnp.int32),
            pltpu.SemaphoreType.DMA((CHUNKS, 5)),
            pltpu.SemaphoreType.DMA(()),
            pltpu.SemaphoreType.DMA((3,)),
            pltpu.SemaphoreType.DMA((3,)),
        ],
        compiler_params=pltpu.CompilerParams(vmem_limit_bytes=VMEM_LIMIT),
        cost_estimate=pl.CostEstimate(flops=30000000, bytes_accessed=12000000, transcendentals=0),
        name="first",
    )(left(dest), left(source), left(window), left(atm), left(ocean), left(weights))


STEPS = 5
PAD = 8
SHIFTED = (3,)


def beyond_columns(gy, mine, v_mine, other, v_other):
    scale, mixing = 0.25 * time_step, time_step * diffusion
    sign = jnp.where(gy == 0, -scale, scale)
    return mixing * other + sign * ((v_mine + v_other) * other + v_other * mine)


def shift_matrix():
    shape = (2 * LANES, 2 * LANES)
    source, to = row_of(shape) % LANES, lane_of(shape)
    left = jnp.where(to < LANES, (to + 1) % LANES, (to + LANES - 1) % LANES)
    return jnp.where(source == left, 1.0, 0.0).astype(jnp.bfloat16)


def shifted_rows(rows, matrix):
    high = rows.astype(jnp.bfloat16)
    low = (rows - high.astype(jnp.float32)).astype(jnp.bfloat16)
    return jnp.dot(jnp.concatenate([high, low], axis=1), matrix, preferred_element_type=jnp.float32)


def step_level(ref, index, shifted, groups, halves, beyond, write):
    lane = lane_of((SUB, LANES))
    first_lane, last_lane = lane == 0, lane == LANES - 1
    scale, mixing = 0.25 * time_step, time_step * diffusion

    def rows(f, h, r, offset):
        return ref[index(f, h) + (pl.ds(PAD + r * SUB + offset, SUB), slice(None))]

    def along_y(f, r, tiles):
        if f in SHIFTED:
            left, right = zip(*[shifted(f, r, h) for h in range(halves)])
            left, right = list(left), list(right)
        else:
            right = [pltpu.roll(t, 1, 1) for t in tiles]
            left = [pltpu.roll(t, LANES - 1, 1) for t in tiles]
        lows = [jnp.where(first_lane, b, t) for b, t in zip([0.0] + right[:-1], right)]
        highs = [jnp.where(last_lane, b, t) for b, t in zip(left[1:] + [0.0], left)]
        return lows, highs

    for r in range(groups):
        q = [[rows(f, h, r, 0) for h in range(halves)] for f in range(2)]
        v = [scale * rows(3, h, r, 0) for h in range(halves)]
        v_low, v_high = along_y(3, r, v)
        sides = [along_y(f, r, q[f]) for f in range(2)]
        for h in range(halves):
            u, u_low, u_high = (scale * rows(2, h, r, offset) for offset in (0, -1, 1))
            centre = (1.0 - 4.0 * mixing) + ((u_low - u_high) + (v_low[h] - v_high[h]))
            x_high, x_low = (mixing - u) - u_high, (mixing + u) + u_low
            y_high, y_low = (mixing - v[h]) - v_high[h], (mixing + v[h]) + v_low[h]
            for f in range(2):
                new = centre * q[f][h] + (x_high * rows(f, h, r, 1) + x_low * rows(f, h, r, -1))
                new = new + (y_high * sides[f][1][h] + y_low * sides[f][0][h])
                write(f, r, h, new + beyond(f, r, h), q[f][h])


def transport_kernel(
    atm_ref,
    ocean_ref,
    some_air_ref,
    land_ref,
    flux_ref,
    first_ref,
    second_ref,
    mine_ref,
    y_ref,
    air_ref,
    sea_ref,
    top_ref,
    air,
    sea,
    air_new,
    sea_new,
    air_edge,
    sea_edge,
    air_shifted,
    sea_shifted,
    matrix,
    in_sems,
    out_sems,
):
    all_air, air_rows = atm_ref.shape[1:3]
    all_sea, sea_rows, sea_cols = ocean_ref.shape[1:]
    a, o = all_air // STEPS, all_sea // STEPS
    halves = sea_cols // LANES
    pitch = padded_levels(all_air)
    even, gy = lax.axis_index("gx") % 2 == 0, lax.axis_index("gy")

    def air_in(step):
        levels = pl.ds(step * a, a)
        yield pltpu.make_async_copy(
            atm_ref.at[:, levels], air.at[:, levels, pl.ds(PAD, air_rows)], in_sems.at[step, halves]
        )

    def sea_in(step):
        levels = pl.ds(step * o, o)
        for h in range(halves):
            yield pltpu.make_async_copy(
                ocean_ref.at[:, levels, :, pl.ds(h * LANES, LANES)],
                sea.at[h, :, levels, pl.ds(PAD, sea_rows)],
                in_sems.at[step, h],
            )

    def air_out(step):
        levels = pl.ds(step * a, a)
        return pltpu.make_async_copy(air_new.at[:, levels], air_ref.at[:, levels], out_sems.at[step, 0])

    def sea_out(step):
        levels = pl.ds(step * o, o)
        return pltpu.make_async_copy(sea_new.at[:, levels], sea_ref.at[:, levels], out_sems.at[step, 1])

    for step in range(STEPS):
        for copy in (*sea_in(step), *(air_in(step) if step > 0 else ())):
            copy.start()
    matrix[...] = shift_matrix()
    air[:, :a, pl.ds(PAD, air_rows), :] = some_air_ref[...]

    lane = lane_of((air_rows, LANES))
    mine, other = mine_ref[:air_rows], y_ref[:air_rows]

    def twice(v):
        return jnp.where(lane < LANES // 2, v, pltpu.roll(v, LANES // 2, 1))

    v_mine, v_other = twice(mine_ref[air_rows : 2 * air_rows]), twice(y_ref[air_rows : 2 * air_rows])
    air_edge[...] = beyond_columns(gy, mine, v_mine, other, v_other)
    lane = lane_of((sea_rows, LANES))
    mine, other = mine_ref[2 * air_rows :], y_ref[2 * air_rows :]

    def both(columns):
        first, second = (pltpu.roll(columns, LANES - n * all_sea, 1) for n in (2, 1))
        return jnp.where(lane < all_sea, first, second)

    sea_edge[...] = beyond_columns(gy, mine, both(mine), other, both(other))

    edge = jnp.where(gy == 0, LANES - 1, 0)
    lane = lane_of((SUB, LANES))
    at_first, at_last = (lane == 0) & (gy != 0), (lane == LANES - 1) & (gy == 0)
    at_edge = lane == edge

    def column(ref, r, at):
        return pltpu.roll(ref[pl.ds(r * SUB, SUB), :], (edge - at + LANES) % LANES, 1)

    def x_rows(at):
        one, other = first_ref[pl.ds(at, 1), :], second_ref[pl.ds(at, 1), :]
        return jnp.where(even, other, one), jnp.where(even, one, other)

    def some_air(step):
        for j in range(a):
            level = step * a + j
            for f in range(3):
                before, after = x_rows(f * pitch + level)
                air[f, level, pl.ds(PAD - 1, 1), :] = before
                air[f, level, pl.ds(PAD + air_rows, 1), :] = after
        for i, f in enumerate(SHIFTED):
            rows = air[f, pl.ds(step * a, a), pl.ds(PAD, air_rows), :].reshape(a * air_rows, LANES)
            air_shifted[i] = shifted_rows((0.25 * time_step if f == 3 else 1.0) * rows, matrix[...])
        stores = []
        for j in range(a):
            level = step * a + j

            def beyond(f, r, h):
                return jnp.where(at_edge, column(air_edge, r, f * (LANES // 2) + level), 0.0)

            def shifted(f, r, h):
                rows = pl.ds(j * air_rows + r * SUB, SUB)
                i = SHIFTED.index(f)
                return air_shifted[i, rows, pl.ds(0, LANES)], air_shifted[i, rows, pl.ds(LANES, LANES)]

            def write(f, r, h, new, q):
                stores.append((f, level, pl.ds(r * SUB, SUB), new))

            step_level(air, lambda f, h: (f, level), shifted, air_rows // SUB, 1, beyond, write)
        for *place, new in stores:
            air_new[tuple(place)] = new

    def some_sea(step):
        for j in range(o):
            level = step * o + j
            for f in range(3):
                for h in range(halves):
                    before, after = x_rows(3 * pitch + (f * halves + h) * all_sea + level)
                    sea[h, f, level, pl.ds(PAD - 1, 1), :] = before
                    sea[h, f, level, pl.ds(PAD + sea_rows, 1), :] = after
        for i, f in enumerate(SHIFTED):
            for h in range(halves):
                rows = sea[h, f, pl.ds(step * o, o), pl.ds(PAD, sea_rows), :].reshape(o * sea_rows, LANES)
                sea_shifted[i, h] = shifted_rows((0.25 * time_step if f == 3 else 1.0) * rows, matrix[...])
        stores = []
        for j in range(o):
            level = step * o + j
            columns = {}

            def beyond(f, r, h):
                if (f, r) not in columns:
                    columns[f, r] = column(sea_edge, r, f * all_sea + level)
                added = columns[f, r]
                if h == 0:
                    return jnp.where(at_first, added, 0.0)
                return jnp.where(at_last, added, 0.0) if h == halves - 1 else 0.0

            def shifted(f, r, h):
                rows = pl.ds(j * sea_rows + r * SUB, SUB)
                i = SHIFTED.index(f)
                return sea_shifted[i, h, rows, pl.ds(0, LANES)], sea_shifted[i, h, rows, pl.ds(LANES, LANES)]

            def write(f, r, h, new, q):
                rows, span = pl.ds(r * SUB, SUB), pl.ds(h * LANES, LANES)
                stores.append((f, level, rows, span, jnp.where(land_ref[rows, span] == 1, new, q)))

            step_level(sea, lambda f, h: (h, f, level), shifted, sea_rows // SUB, halves, beyond, write)
        for *place, new in stores:
            sea_new[tuple(place)] = new

    some_air(0)
    for f in range(2):
        air_new[f, 0] = air_new[f, 0] + time_step * flux_ref[f]
    air_out(0).start()

    def some_levels(step, carry):
        for copy in sea_in(step):
            copy.wait()
        some_sea(step)
        sea_out(step).start()

        @pl.when(step == 0)
        def _():
            top_ref[...] = sea_new[:, 0]

        @pl.when(step > 0)
        def _():
            for copy in air_in(step):
                copy.wait()
            some_air(step)
            air_out(step).start()

        return carry

    lax.fori_loop(0, STEPS, some_levels, 0)
    for step in range(STEPS):
        air_out(step).wait()
        sea_out(step).wait()


def transport(atm, ocean, some_air, land, flux, first_rows, second_rows, mine, y):
    air_levels, air_rows, _ = atm.shape[1:]
    sea_levels, sea_rows, sea_cols = ocean.shape[1:]
    halves = sea_cols // LANES
    vmem = pl.BlockSpec(memory_space=pltpu.VMEM)
    hbm = pl.BlockSpec(memory_space=pltpu.HBM)
    air_shape, sea_shape = (2,) + atm.shape[1:], (2,) + ocean.shape[1:]
    return pl.pallas_call(
        transport_kernel,
        in_specs=[hbm, hbm] + [vmem] * 7,
        out_specs=[hbm, hbm, vmem],
        out_shape=(
            jax.ShapeDtypeStruct(air_shape, jnp.float32),
            jax.ShapeDtypeStruct(sea_shape, jnp.float32),
            pltpu.VMEM((2, sea_rows, sea_cols), jnp.float32),
        ),
        scratch_shapes=[
            pltpu.VMEM((4, air_levels, air_rows + 2 * PAD, LANES), jnp.float32),
            pltpu.VMEM((halves, 4, sea_levels, sea_rows + 2 * PAD, LANES), jnp.float32),
            pltpu.VMEM(air_shape, jnp.float32),
            pltpu.VMEM(sea_shape, jnp.float32),
            pltpu.VMEM((air_rows, LANES), jnp.float32),
            pltpu.VMEM((sea_rows, LANES), jnp.float32),
            pltpu.VMEM((len(SHIFTED), air_levels // STEPS * air_rows, 2 * LANES), jnp.float32),
            pltpu.VMEM((len(SHIFTED), halves, sea_levels // STEPS * sea_rows, 2 * LANES), jnp.float32),
            pltpu.VMEM((2 * LANES, 2 * LANES), jnp.bfloat16),
            pltpu.SemaphoreType.DMA((STEPS, halves + 1)),
            pltpu.SemaphoreType.DMA((STEPS, 2)),
        ],
        compiler_params=pltpu.CompilerParams(vmem_limit_bytes=VMEM_LIMIT),
        cost_estimate=pl.CostEstimate(flops=60000000, bytes_accessed=22000000, transcendentals=0),
        name="transport",
    )(left(atm), left(ocean), some_air, held(land), flux, held(first_rows), held(second_rows), mine, held(y))


def body(
    atm_fields,
    ocean_fields,
    land_sea,
    sea_weights,
    sea_dest,
    sea_source,
    sea_window,
    air_weights,
    air_dest,
    air_source,
    air_window,
):
    width_x, width_y = lax.axis_size("gx"), lax.axis_size("gy")
    assert width_y == 2 and width_x % 2 == 0
    tiles = width_x * width_y
    exchange = functools.partial(lax.all_to_all, axis_name=("gx", "gy"), split_axis=0, concat_axis=0, tiled=True)
    pairs = [(i, i ^ 1) for i in range(width_x)]
    other_pairs = [(i, (i + 1 if i % 2 else i - 1) % width_x) for i in range(width_x)]

    to_air, rows, other_rows, mine, some_air = first(
        tiles, atm_fields, ocean_fields, sea_weights, sea_dest.reshape(-1), sea_source, sea_window
    )
    on_air = exchange(to_air)
    side = lax.ppermute(mine, "gy", [(0, 1), (1, 0)])
    rows = lax.ppermute(rows, "gx", pairs)
    other_rows = lax.ppermute(other_rows, "gx", other_pairs)
    to_sea, fluxes = air_send(on_air, some_air, air_weights, air_dest.reshape(-1), air_source, air_window)
    to_sea, side = lax.optimization_barrier((to_sea, side))
    on_sea = exchange(to_sea)
    air_next, sea_next, top = transport(
        atm_fields, ocean_fields, some_air, land_sea, fluxes, rows, other_rows, mine, side
    )
    sea_next = add_sea_forcing(on_sea, land_sea, top, sea_next)
    return (air_next, sea_next)


def solution(mesh):
    placed = (
        P("ens", None, "gx", "gy"),
        P("ens", None, "gx", "gy"),
        P(("ens", "gx"), "gy"),
        P(("ens", "gx", "gy"), None, None),
        P(("ens", "gx", "gy"), None),
        P(("ens", "gx", "gy")),
        P(("ens", "gx", "gy")),
        P(("ens", "gx", "gy"), None, None),
        P(("ens", "gx", "gy"), None),
        P(("ens", "gx", "gy")),
        P(("ens", "gx", "gy")),
    )
    return jax.shard_map(
        body,
        mesh=mesh,
        in_specs=placed,
        out_specs=(P("ens", None, "gx", "gy"), P("ens", None, "gx", "gy")),
        check_vma=False,
    )
```

```python
import functools

import jax
import jax.numpy as jnp
from jax import lax
from jax.experimental import pallas as pl
from jax.experimental.pallas import tpu as pltpu
from jax.sharding import PartitionSpec as P

WIN = 128
CAP = 2
ROWS = 4
LANES = 128
SUB = 8

time_step = 0.1
diffusion = 0.2
VMEM_LIMIT = 40 * 1024 * 1024


def held(array):
    return pltpu.with_memory_space_constraint(array, pltpu.VMEM)


def left(array):
    return pltpu.with_memory_space_constraint(array, pltpu.HBM)


def lane_of(shape):
    return lax.broadcasted_iota(jnp.int32, shape, len(shape) - 1)


def row_of(shape):
    return lax.broadcasted_iota(jnp.int32, shape, len(shape) - 2)


def send_blocks(pick, count, weights_ref, dest_ref, window_ref, picked_ref, counts_ref, out_ref):
    blocks = weights_ref.shape[0]
    out_ref[...] = jnp.zeros_like(out_ref)

    def clear(d, carry):
        counts_ref[d] = 0
        return carry

    lax.fori_loop(0, out_ref.shape[0], clear, 0)
    picked_ref[...] = jnp.zeros_like(picked_ref)
    for k in range(blocks):
        for f in range(count):
            picked_ref[k, pl.ds(f, 1), :] = pick(k, f)
    row = row_of((SUB, LANES))
    lane = lane_of((SUB, LANES))
    for k in range(blocks):
        values = picked_ref[k]
        high = values.astype(jnp.bfloat16)
        low = (values - high.astype(jnp.float32)).astype(jnp.bfloat16)
        left = jnp.concatenate([high.astype(jnp.float32), low.astype(jnp.float32)], axis=0).astype(jnp.bfloat16)
        weight = weights_ref[k]
        weight_high = weight.astype(jnp.bfloat16)
        weight_low = (weight - weight_high.astype(jnp.float32)).astype(jnp.bfloat16)
        right = jnp.concatenate([weight_high, weight_low], axis=0)
        product = lax.dot_general(left, right, (((1,), (1,)), ((), ())), preferred_element_type=jnp.float32)
        total = product[:SUB, :WIN] + (product[SUB:, :WIN] + product[:SUB, WIN:])
        d = dest_ref[k]
        slot = counts_ref[d]
        counts_ref[d] = slot + 1
        onehot = jnp.where(lane == window_ref[k], 1.0, 0.0)
        total = jnp.where(row == ROWS - 1, onehot, jnp.where(row < count, total, 0.0))
        total = jnp.where(slot == 0, total, jnp.concatenate([total[ROWS:], total[:ROWS]], axis=0))
        out_ref[d] = out_ref[d] + total


def receive_blocks(arrived_ref, count):
    slots = arrived_ref.shape[0] // ROWS
    onehot = arrived_ref[pl.ds(ROWS - 1, slots, stride=ROWS), :]
    fields = [arrived_ref[pl.ds(f, slots, stride=ROWS), :] for f in range(count)]
    return [
        lax.dot_general(
            onehot, field, (((0,), (0,)), ((), ())), precision=lax.Precision.HIGHEST, preferred_element_type=jnp.float32
        )
        for field in fields
    ]


def index_copies(refs, held_refs, sems):
    return [pltpu.make_async_copy(src, dst, sems.at[i]) for i, (src, dst) in enumerate(zip(refs, held_refs))]


def air_send_kernel(
    dest_hbm,
    source_hbm,
    window_hbm,
    arrived_ref,
    some_air_ref,
    weights_ref,
    out_ref,
    flux_ref,
    picked_ref,
    counts_ref,
    dest_ref,
    source_ref,
    window_ref,
    sems,
):
    indices = index_copies((dest_hbm, source_hbm, window_hbm), (dest_ref, source_ref, window_ref), sems)
    for copy in indices:
        copy.start()
    rows = some_air_ref.shape[2]
    surface = [some_air_ref[f, 0] for f in range(4)]
    on_air = [field[:rows] for field in receive_blocks(arrived_ref, 3)]
    relative_u = surface[2] - on_air[1]
    relative_v = surface[3] - on_air[2]
    wind_speed = jnp.sqrt(relative_u * relative_u + relative_v * relative_v + 1.0)
    flux_ref[0] = 0.5 * wind_speed * (on_air[0] - surface[0])
    flux_ref[1] = 0.4 * wind_speed * (0.8 * on_air[0] - surface[1])

    for copy in indices:
        copy.wait()

    def pick(k, f):
        return flux_ref[f, pl.ds(source_ref[k], 1), :]

    send_blocks(pick, 2, weights_ref, dest_ref, window_ref, picked_ref, counts_ref, out_ref)


def air_send(arrived, some_air, weights, dest, source, window):
    blocks = weights.shape[0]
    tiles = arrived.shape[0]
    vmem = pl.BlockSpec(memory_space=pltpu.VMEM)
    hbm = pl.BlockSpec(memory_space=pltpu.HBM)
    return pl.pallas_call(
        air_send_kernel,
        in_specs=[hbm] * 3 + [vmem] * 3,
        out_specs=(vmem, vmem),
        out_shape=(
            pltpu.VMEM((tiles, CAP * ROWS, WIN), jnp.float32),
            pltpu.VMEM((2,) + some_air.shape[2:], jnp.float32),
        ),
        scratch_shapes=[pltpu.VMEM((blocks, SUB, WIN), jnp.float32), pltpu.SMEM((tiles,), jnp.int32)]
        + [pltpu.SMEM((blocks,), jnp.int32)] * 3
        + [pltpu.SemaphoreType.DMA((3,))],
        compiler_params=pltpu.CompilerParams(vmem_limit_bytes=VMEM_LIMIT),
        cost_estimate=pl.CostEstimate(flops=blocks * 2 * 16 * 128 * 256, bytes_accessed=2000000, transcendentals=0),
        name="air_send",
    )(
        left(dest),
        left(source),
        left(window),
        held(arrived.reshape(tiles * CAP * ROWS, WIN)),
        some_air,
        held(weights),
    )


def sea_forcing_kernel(arrived_ref, land_ref, top_ref, before_ref, after_ref, summed_ref, new_ref, sem):
    del before_ref
    rows, cols = land_ref.shape
    halves = cols // WIN
    for f, field in enumerate(receive_blocks(arrived_ref, 2)):
        summed_ref[f] = field
        for h in range(halves):
            span = pl.ds(h * WIN, WIN)
            forcing = summed_ref[f, pl.ds(h, rows, stride=halves), :] * (-0.5, 0.3)[f]
            change = jnp.where(land_ref[:, span] == 1, time_step * forcing, 0.0)
            new_ref[f, :, span] = top_ref[f, :, span] + change
    copy = pltpu.make_async_copy(new_ref, after_ref.at[:, 0], sem)
    copy.start()
    copy.wait()


def add_sea_forcing(arrived, land, top, sea_next):
    tiles = arrived.shape[0]
    rows, cols = land.shape
    vmem = pl.BlockSpec(memory_space=pltpu.VMEM)
    hbm = pl.BlockSpec(memory_space=pltpu.HBM)
    return pl.pallas_call(
        sea_forcing_kernel,
        in_specs=[vmem, vmem, vmem, hbm],
        out_specs=hbm,
        out_shape=jax.ShapeDtypeStruct(sea_next.shape, jnp.float32),
        scratch_shapes=[
            pltpu.VMEM((2, rows * cols // WIN, WIN), jnp.float32),
            pltpu.VMEM((2, rows, cols), jnp.float32),
            pltpu.SemaphoreType.DMA(()),
        ],
        input_output_aliases={3: 0},
        compiler_params=pltpu.CompilerParams(vmem_limit_bytes=VMEM_LIMIT),
        cost_estimate=pl.CostEstimate(flops=4000000, bytes_accessed=600000, transcendentals=0),
        name="sea_forcing",
    )(held(arrived.reshape(tiles * CAP * ROWS, WIN)), held(land), top, sea_next)


def padded_levels(levels):
    return -(-levels // SUB) * SUB


CHUNKS = 4


def first_kernel(
    dest_hbm,
    source_hbm,
    window_hbm,
    atm_ref,
    ocean_ref,
    weights_ref,
    out_ref,
    first_ref,
    second_ref,
    y_ref,
    some_air_ref,
    air,
    sea,
    sea_v,
    low,
    high,
    weights,
    top,
    windows,
    picked,
    counts,
    dest_ref,
    source_ref,
    window_ref,
    sems,
    weight_sems,
    top_sems,
    index_sems,
):
    air_levels, air_rows = atm_ref.shape[1:3]
    sea_levels, sea_rows, sea_cols = ocean_ref.shape[1:]
    halves = sea_cols // WIN
    pitch = padded_levels(air_levels)
    gx, gy, last_gx = lax.axis_index("gx"), lax.axis_index("gy"), lax.axis_size("gx") - 1
    even = gx % 2 == 0
    at_end = (gx == 0) | (gx == last_gx)
    edge = jnp.where(gy == 0, LANES - 1, 0)
    span = pl.ds(pl.multiple_of(jnp.where(gy == 0, sea_cols - LANES, 0), LANES), LANES)
    a, o = air_levels // CHUNKS, sea_levels // CHUNKS

    tops = [pltpu.make_async_copy(ocean_ref.at[f, 0], top.at[i], top_sems.at[i]) for i, f in enumerate((0, 2, 3))]
    weights_in = pltpu.make_async_copy(weights_ref, weights, weight_sems)

    def copies(chunk):
        air_span, sea_span = pl.ds(chunk * a, a), pl.ds(chunk * o, o)
        pairs = [
            (atm_ref.at[:, air_span], air.at[:, air_span]),
            (ocean_ref.at[pl.ds(0, 2), sea_span, :, span], sea.at[:, sea_span]),
            (ocean_ref.at[3, sea_span, :, span], sea_v.at[sea_span]),
            (ocean_ref.at[pl.ds(0, 3), sea_span, pl.ds(0, SUB)], low.at[:, sea_span]),
            (ocean_ref.at[pl.ds(0, 3), sea_span, pl.ds(sea_rows - SUB, SUB)], high.at[:, sea_span]),
        ]
        return [pltpu.make_async_copy(src, dst, sems.at[chunk, i]) for i, (src, dst) in enumerate(pairs)]

    indices = index_copies((dest_hbm, source_hbm, window_hbm), (dest_ref, source_ref, window_ref), index_sems)
    for copy in indices + tops:
        copy.start()
    weights_in.start()
    for chunk in range(CHUNKS):
        for copy in copies(chunk):
            copy.start()

    for copy in indices + tops:
        copy.wait()
    for f in range(3):
        for h in range(halves):
            windows[f, pl.ds(h, sea_rows, stride=halves), :] = top[f, :, pl.ds(h * WIN, WIN)]
    weights_in.wait()

    def pick(k, f):
        return windows[f, pl.ds(source_ref[k], 1), :]

    send_blocks(pick, 3, weights, dest_ref, window_ref, picked, counts, out_ref)

    for f in range(3):
        for ref in (first_ref, second_ref):
            ref[pl.ds((f + 1) * pitch - SUB, SUB), :] = jnp.zeros((SUB, LANES), jnp.float32)

    def put_rows(to, low_row, high_row):
        first_ref[pl.ds(to, 1), :] = jnp.where(even, high_row, low_row)
        second_ref[pl.ds(to, 1), :] = jnp.where(at_end, 0.0, jnp.where(even, low_row, high_row))

    def put(total, column, to, lane):
        return jnp.where(lane == to, pltpu.roll(column, (to - edge + LANES) % LANES, 1), total)

    air_lane, sea_lane = lane_of((air_rows, LANES)), lane_of((sea_rows, LANES))
    tracers = v = jnp.zeros((air_rows, LANES), jnp.float32)
    total = jnp.zeros((sea_rows, LANES), jnp.float32)
    for chunk in range(CHUNKS):
        for copy in copies(chunk):
            copy.wait()
        if chunk == 0:
            some_air_ref[...] = air[:, : some_air_ref.shape[1]]
        for level in range(chunk * a, (chunk + 1) * a):
            tracers = put(tracers, air[0, level], level, air_lane)
            tracers = put(tracers, air[1, level], LANES // 2 + level, air_lane)
            v = put(v, air[3, level], level, air_lane)
            for f in range(3):
                put_rows(f * pitch + level, air[f, level, pl.ds(0, 1), :], air[f, level, pl.ds(air_rows - 1, 1), :])
        for level in range(chunk * o, (chunk + 1) * o):
            total = put(total, sea[0, level], level, sea_lane)
            total = put(total, sea[1, level], sea_levels + level, sea_lane)
            total = put(total, sea_v[level], 2 * sea_levels + level, sea_lane)
            for f in range(3):
                for h in range(halves):
                    tile = pl.ds(h * WIN, WIN)
                    put_rows(
                        3 * pitch + (f * halves + h) * sea_levels + level,
                        low[f, level, pl.ds(0, 1), tile],
                        high[f, level, pl.ds(SUB - 1, 1), tile],
                    )
    y_ref[:air_rows] = tracers
    y_ref[air_rows : 2 * air_rows] = v
    y_ref[2 * air_rows :] = total


def first(tiles, atm, ocean, weights, dest, source, window):
    blocks = weights.shape[0]
    air_levels, air_rows, _ = atm.shape[1:]
    sea_levels, sea_rows, sea_cols = ocean.shape[1:]
    xrows = 3 * padded_levels(air_levels) + 3 * sea_levels * (sea_cols // WIN)
    yrows = 2 * air_rows + sea_rows
    vmem = pl.BlockSpec(memory_space=pltpu.VMEM)
    hbm = pl.BlockSpec(memory_space=pltpu.HBM)
    return pl.pallas_call(
        first_kernel,
        in_specs=[hbm] * 6,
        out_specs=[vmem] * 5,
        out_shape=(
            pltpu.VMEM((tiles, CAP * ROWS, WIN), jnp.float32),
            pltpu.VMEM((xrows, LANES), jnp.float32),
            pltpu.VMEM((xrows, LANES), jnp.float32),
            pltpu.VMEM((yrows, LANES), jnp.float32),
            pltpu.VMEM((4, air_levels // STEPS, air_rows, LANES), jnp.float32),
        ),
        scratch_shapes=[
            pltpu.VMEM(atm.shape, jnp.float32),
            pltpu.VMEM((2, sea_levels, sea_rows, LANES), jnp.float32),
            pltpu.VMEM((sea_levels, sea_rows, LANES), jnp.float32),
            pltpu.VMEM((3, sea_levels, SUB, sea_cols), jnp.float32),
            pltpu.VMEM((3, sea_levels, SUB, sea_cols), jnp.float32),
            pltpu.VMEM(weights.shape, jnp.float32),
            pltpu.VMEM((3, sea_rows, sea_cols), jnp.float32),
            pltpu.VMEM((3, sea_rows * sea_cols // WIN, WIN), jnp.float32),
            pltpu.VMEM((blocks, SUB, WIN), jnp.float32),
            pltpu.SMEM((tiles,), jnp.int32),
            pltpu.SMEM((blocks,), jnp.int32),
            pltpu.SMEM((blocks,), jnp.int32),
            pltpu.SMEM((blocks,), jnp.int32),
            pltpu.SemaphoreType.DMA((CHUNKS, 5)),
            pltpu.SemaphoreType.DMA(()),
            pltpu.SemaphoreType.DMA((3,)),
            pltpu.SemaphoreType.DMA((3,)),
        ],
        compiler_params=pltpu.CompilerParams(vmem_limit_bytes=VMEM_LIMIT),
        cost_estimate=pl.CostEstimate(flops=30000000, bytes_accessed=12000000, transcendentals=0),
        name="first",
    )(left(dest), left(source), left(window), left(atm), left(ocean), left(weights))


STEPS = 5
PAD = 8
SHIFTED = (3,)


def beyond_columns(gy, mine, v_mine, other, v_other):
    scale, mixing = 0.25 * time_step, time_step * diffusion
    sign = jnp.where(gy == 0, -scale, scale)
    return mixing * other + sign * ((v_mine + v_other) * other + v_other * mine)


def shift_matrix():
    shape = (2 * LANES, 2 * LANES)
    source, to = row_of(shape) % LANES, lane_of(shape)
    left = jnp.where(to < LANES, (to + 1) % LANES, (to + LANES - 1) % LANES)
    return jnp.where(source == left, 1.0, 0.0).astype(jnp.bfloat16)


def shifted_rows(rows, matrix):
    high = rows.astype(jnp.bfloat16)
    low = (rows - high.astype(jnp.float32)).astype(jnp.bfloat16)
    return jnp.dot(jnp.concatenate([high, low], axis=1), matrix, preferred_element_type=jnp.float32)


def step_level(ref, index, shifted, groups, halves, beyond, write):
    lane = lane_of((SUB, LANES))
    first_lane, last_lane = lane == 0, lane == LANES - 1
    scale, mixing = 0.25 * time_step, time_step * diffusion

    def rows(f, h, r, offset):
        return ref[index(f, h) + (pl.ds(PAD + r * SUB + offset, SUB), slice(None))]

    def along_y(f, r, tiles):
        if f in SHIFTED:
            left, right = zip(*[shifted(f, r, h) for h in range(halves)])
            left, right = list(left), list(right)
        else:
            right = [pltpu.roll(t, 1, 1) for t in tiles]
            left = [pltpu.roll(t, LANES - 1, 1) for t in tiles]
        lows = [jnp.where(first_lane, b, t) for b, t in zip([0.0] + right[:-1], right)]
        highs = [jnp.where(last_lane, b, t) for b, t in zip(left[1:] + [0.0], left)]
        return lows, highs

    for r in range(groups):
        q = [[rows(f, h, r, 0) for h in range(halves)] for f in range(2)]
        v = [scale * rows(3, h, r, 0) for h in range(halves)]
        v_low, v_high = along_y(3, r, v)
        sides = [along_y(f, r, q[f]) for f in range(2)]
        for h in range(halves):
            u, u_low, u_high = (scale * rows(2, h, r, offset) for offset in (0, -1, 1))
            centre = (1.0 - 4.0 * mixing) + ((u_low - u_high) + (v_low[h] - v_high[h]))
            x_high, x_low = (mixing - u) - u_high, (mixing + u) + u_low
            y_high, y_low = (mixing - v[h]) - v_high[h], (mixing + v[h]) + v_low[h]
            for f in range(2):
                new = centre * q[f][h] + (x_high * rows(f, h, r, 1) + x_low * rows(f, h, r, -1))
                new = new + (y_high * sides[f][1][h] + y_low * sides[f][0][h])
                write(f, r, h, new + beyond(f, r, h), q[f][h])


def transport_kernel(
    atm_ref,
    ocean_ref,
    some_air_ref,
    land_ref,
    flux_ref,
    first_ref,
    second_ref,
    mine_ref,
    y_ref,
    air_ref,
    sea_ref,
    top_ref,
    air,
    sea,
    air_new,
    sea_new,
    air_edge,
    sea_edge,
    air_shifted,
    sea_shifted,
    matrix,
    in_sems,
    out_sems,
):
    all_air, air_rows = atm_ref.shape[1:3]
    all_sea, sea_rows, sea_cols = ocean_ref.shape[1:]
    a, o = all_air // STEPS, all_sea // STEPS
    halves = sea_cols // LANES
    pitch = padded_levels(all_air)
    even, gy = lax.axis_index("gx") % 2 == 0, lax.axis_index("gy")

    def air_in(step):
        levels = pl.ds(step * a, a)
        yield pltpu.make_async_copy(
            atm_ref.at[:, levels], air.at[:, levels, pl.ds(PAD, air_rows)], in_sems.at[step, halves]
        )

    def sea_in(step):
        levels = pl.ds(step * o, o)
        for h in range(halves):
            yield pltpu.make_async_copy(
                ocean_ref.at[:, levels, :, pl.ds(h * LANES, LANES)],
                sea.at[h, :, levels, pl.ds(PAD, sea_rows)],
                in_sems.at[step, h],
            )

    def air_out(step):
        levels = pl.ds(step * a, a)
        return pltpu.make_async_copy(air_new.at[:, levels], air_ref.at[:, levels], out_sems.at[step, 0])

    def sea_out(step):
        levels = pl.ds(step * o, o)
        return pltpu.make_async_copy(sea_new.at[:, levels], sea_ref.at[:, levels], out_sems.at[step, 1])

    for step in range(STEPS):
        for copy in (*sea_in(step), *(air_in(step) if step > 0 else ())):
            copy.start()
    matrix[...] = shift_matrix()
    air[:, :a, pl.ds(PAD, air_rows), :] = some_air_ref[...]

    lane = lane_of((air_rows, LANES))
    mine, other = mine_ref[:air_rows], y_ref[:air_rows]

    def twice(v):
        return jnp.where(lane < LANES // 2, v, pltpu.roll(v, LANES // 2, 1))

    v_mine, v_other = twice(mine_ref[air_rows : 2 * air_rows]), twice(y_ref[air_rows : 2 * air_rows])
    air_edge[...] = beyond_columns(gy, mine, v_mine, other, v_other)
    lane = lane_of((sea_rows, LANES))
    mine, other = mine_ref[2 * air_rows :], y_ref[2 * air_rows :]

    def both(columns):
        first, second = (pltpu.roll(columns, LANES - n * all_sea, 1) for n in (2, 1))
        return jnp.where(lane < all_sea, first, second)

    sea_edge[...] = beyond_columns(gy, mine, both(mine), other, both(other))

    edge = jnp.where(gy == 0, LANES - 1, 0)
    lane = lane_of((SUB, LANES))
    at_first, at_last = (lane == 0) & (gy != 0), (lane == LANES - 1) & (gy == 0)
    at_edge = lane == edge

    def column(ref, r, at):
        return pltpu.roll(ref[pl.ds(r * SUB, SUB), :], (edge - at + LANES) % LANES, 1)

    def x_rows(at):
        one, other = first_ref[pl.ds(at, 1), :], second_ref[pl.ds(at, 1), :]
        return jnp.where(even, other, one), jnp.where(even, one, other)

    def some_air(step):
        for j in range(a):
            level = step * a + j
            for f in range(3):
                before, after = x_rows(f * pitch + level)
                air[f, level, pl.ds(PAD - 1, 1), :] = before
                air[f, level, pl.ds(PAD + air_rows, 1), :] = after
        for i, f in enumerate(SHIFTED):
            rows = air[f, pl.ds(step * a, a), pl.ds(PAD, air_rows), :].reshape(a * air_rows, LANES)
            air_shifted[i] = shifted_rows((0.25 * time_step if f == 3 else 1.0) * rows, matrix[...])
        stores = []
        for j in range(a):
            level = step * a + j

            def beyond(f, r, h):
                return jnp.where(at_edge, column(air_edge, r, f * (LANES // 2) + level), 0.0)

            def shifted(f, r, h):
                rows = pl.ds(j * air_rows + r * SUB, SUB)
                i = SHIFTED.index(f)
                return air_shifted[i, rows, pl.ds(0, LANES)], air_shifted[i, rows, pl.ds(LANES, LANES)]

            def write(f, r, h, new, q):
                stores.append((f, level, pl.ds(r * SUB, SUB), new))

            step_level(air, lambda f, h: (f, level), shifted, air_rows // SUB, 1, beyond, write)
        for *place, new in stores:
            air_new[tuple(place)] = new

    def some_sea(step):
        for j in range(o):
            level = step * o + j
            for f in range(3):
                for h in range(halves):
                    before, after = x_rows(3 * pitch + (f * halves + h) * all_sea + level)
                    sea[h, f, level, pl.ds(PAD - 1, 1), :] = before
                    sea[h, f, level, pl.ds(PAD + sea_rows, 1), :] = after
        for i, f in enumerate(SHIFTED):
            for h in range(halves):
                rows = sea[h, f, pl.ds(step * o, o), pl.ds(PAD, sea_rows), :].reshape(o * sea_rows, LANES)
                sea_shifted[i, h] = shifted_rows((0.25 * time_step if f == 3 else 1.0) * rows, matrix[...])
        stores = []
        for j in range(o):
            level = step * o + j
            columns = {}

            def beyond(f, r, h):
                if (f, r) not in columns:
                    columns[f, r] = column(sea_edge, r, f * all_sea + level)
                added = columns[f, r]
                if h == 0:
                    return jnp.where(at_first, added, 0.0)
                return jnp.where(at_last, added, 0.0) if h == halves - 1 else 0.0

            def shifted(f, r, h):
                rows = pl.ds(j * sea_rows + r * SUB, SUB)
                i = SHIFTED.index(f)
                return sea_shifted[i, h, rows, pl.ds(0, LANES)], sea_shifted[i, h, rows, pl.ds(LANES, LANES)]

            def write(f, r, h, new, q):
                rows, span = pl.ds(r * SUB, SUB), pl.ds(h * LANES, LANES)
                stores.append((f, level, rows, span, jnp.where(land_ref[rows, span] == 1, new, q)))

            step_level(sea, lambda f, h: (h, f, level), shifted, sea_rows // SUB, halves, beyond, write)
        for *place, new in stores:
            sea_new[tuple(place)] = new

    some_air(0)
    for f in range(2):
        air_new[f, 0] = air_new[f, 0] + time_step * flux_ref[f]
    air_out(0).start()

    def some_levels(step, carry):
        for copy in sea_in(step):
            copy.wait()
        some_sea(step)
        sea_out(step).start()

        @pl.when(step == 0)
        def _():
            top_ref[...] = sea_new[:, 0]

        @pl.when(step > 0)
        def _():
            for copy in air_in(step):
                copy.wait()
            some_air(step)
            air_out(step).start()

        return carry

    lax.fori_loop(0, STEPS, some_levels, 0)
    for step in range(STEPS):
        air_out(step).wait()
        sea_out(step).wait()


def transport(atm, ocean, some_air, land, flux, first_rows, second_rows, mine, y):
    air_levels, air_rows, _ = atm.shape[1:]
    sea_levels, sea_rows, sea_cols = ocean.shape[1:]
    halves = sea_cols // LANES
    vmem = pl.BlockSpec(memory_space=pltpu.VMEM)
    hbm = pl.BlockSpec(memory_space=pltpu.HBM)
    air_shape, sea_shape = (2,) + atm.shape[1:], (2,) + ocean.shape[1:]
    return pl.pallas_call(
        transport_kernel,
        in_specs=[hbm, hbm] + [vmem] * 7,
        out_specs=[hbm, hbm, vmem],
        out_shape=(
            jax.ShapeDtypeStruct(air_shape, jnp.float32),
            jax.ShapeDtypeStruct(sea_shape, jnp.float32),
            pltpu.VMEM((2, sea_rows, sea_cols), jnp.float32),
        ),
        scratch_shapes=[
            pltpu.VMEM((4, air_levels, air_rows + 2 * PAD, LANES), jnp.float32),
            pltpu.VMEM((halves, 4, sea_levels, sea_rows + 2 * PAD, LANES), jnp.float32),
            pltpu.VMEM(air_shape, jnp.float32),
            pltpu.VMEM(sea_shape, jnp.float32),
            pltpu.VMEM((air_rows, LANES), jnp.float32),
            pltpu.VMEM((sea_rows, LANES), jnp.float32),
            pltpu.VMEM((len(SHIFTED), air_levels // STEPS * air_rows, 2 * LANES), jnp.float32),
            pltpu.VMEM((len(SHIFTED), halves, sea_levels // STEPS * sea_rows, 2 * LANES), jnp.float32),
            pltpu.VMEM((2 * LANES, 2 * LANES), jnp.bfloat16),
            pltpu.SemaphoreType.DMA((STEPS, halves + 1)),
            pltpu.SemaphoreType.DMA((STEPS, 2)),
        ],
        compiler_params=pltpu.CompilerParams(vmem_limit_bytes=VMEM_LIMIT),
        cost_estimate=pl.CostEstimate(flops=60000000, bytes_accessed=22000000, transcendentals=0),
        name="transport",
    )(left(atm), left(ocean), some_air, held(land), flux, held(first_rows), held(second_rows), mine, held(y))


def body(
    atm_fields,
    ocean_fields,
    land_sea,
    sea_weights,
    sea_dest,
    sea_source,
    sea_window,
    air_weights,
    air_dest,
    air_source,
    air_window,
):
    width_x, width_y = lax.axis_size("gx"), lax.axis_size("gy")
    assert width_y == 2 and width_x % 2 == 0
    tiles = width_x * width_y
    exchange = functools.partial(lax.all_to_all, axis_name=("gx", "gy"), split_axis=0, concat_axis=0, tiled=True)
    pairs = [(i, i ^ 1) for i in range(width_x)]
    other_pairs = [(i, i + 1 if i % 2 else i - 1) for i in range(1, width_x - 1)]

    to_air, rows, other_rows, mine, some_air = first(
        tiles, atm_fields, ocean_fields, sea_weights, sea_dest.reshape(-1), sea_source, sea_window
    )
    on_air = exchange(to_air)
    side = lax.ppermute(mine, "gy", [(0, 1), (1, 0)])
    rows = lax.ppermute(rows, "gx", pairs)
    other_rows = lax.ppermute(other_rows, "gx", other_pairs)
    to_sea, fluxes = air_send(on_air, some_air, air_weights, air_dest.reshape(-1), air_source, air_window)
    to_sea, side = lax.optimization_barrier((to_sea, side))
    on_sea = exchange(to_sea)
    air_next, sea_next, top = transport(
        atm_fields, ocean_fields, some_air, land_sea, fluxes, rows, other_rows, mine, side
    )
    sea_next = add_sea_forcing(on_sea, land_sea, top, sea_next)
    return (air_next, sea_next)


def solution(mesh):
    placed = (
        P("ens", None, "gx", "gy"),
        P("ens", None, "gx", "gy"),
        P(("ens", "gx"), "gy"),
        P(("ens", "gx", "gy"), None, None),
        P(("ens", "gx", "gy"), None),
        P(("ens", "gx", "gy")),
        P(("ens", "gx", "gy")),
        P(("ens", "gx", "gy"), None, None),
        P(("ens", "gx", "gy"), None),
        P(("ens", "gx", "gy")),
        P(("ens", "gx", "gy")),
    )
    return jax.shard_map(
        body,
        mesh=mesh,
        in_specs=placed,
        out_specs=(P("ens", None, "gx", "gy"), P("ens", None, "gx", "gy")),
        check_vma=False,
    )
```

```python
import functools

import jax
import jax.numpy as jnp
from jax import lax
from jax.experimental import pallas as pl
from jax.experimental.pallas import tpu as pltpu
from jax.sharding import PartitionSpec as P

WIN = 128
CAP = 2
ROWS = 4
LANES = 128
SUB = 8

time_step = 0.1
diffusion = 0.2
VMEM_LIMIT = 40 * 1024 * 1024


def held(array):
    return pltpu.with_memory_space_constraint(array, pltpu.VMEM)


def left(array):
    return pltpu.with_memory_space_constraint(array, pltpu.HBM)


def lane_of(shape):
    return lax.broadcasted_iota(jnp.int32, shape, len(shape) - 1)


def row_of(shape):
    return lax.broadcasted_iota(jnp.int32, shape, len(shape) - 2)


def send_blocks(pick, count, weights_ref, dest_ref, window_ref, picked_ref, counts_ref, out_ref):
    blocks = weights_ref.shape[0]
    out_ref[...] = jnp.zeros_like(out_ref)

    def clear(d, carry):
        counts_ref[d] = 0
        return carry

    lax.fori_loop(0, out_ref.shape[0], clear, 0)
    picked_ref[...] = jnp.zeros_like(picked_ref)
    for k in range(blocks):
        for f in range(count):
            picked_ref[k, pl.ds(f, 1), :] = pick(k, f)
    row = row_of((SUB, LANES))
    lane = lane_of((SUB, LANES))
    for k in range(blocks):
        values = picked_ref[k]
        high = values.astype(jnp.bfloat16)
        low = (values - high.astype(jnp.float32)).astype(jnp.bfloat16)
        left = jnp.concatenate([high.astype(jnp.float32), low.astype(jnp.float32)], axis=0).astype(jnp.bfloat16)
        weight = weights_ref[k]
        weight_high = weight.astype(jnp.bfloat16)
        weight_low = (weight - weight_high.astype(jnp.float32)).astype(jnp.bfloat16)
        right = jnp.concatenate([weight_high, weight_low], axis=0)
        product = lax.dot_general(left, right, (((1,), (1,)), ((), ())), preferred_element_type=jnp.float32)
        total = product[:SUB, :WIN] + (product[SUB:, :WIN] + product[:SUB, WIN:])
        d = dest_ref[k]
        slot = counts_ref[d]
        counts_ref[d] = slot + 1
        onehot = jnp.where(lane == window_ref[k], 1.0, 0.0)
        total = jnp.where(row == ROWS - 1, onehot, jnp.where(row < count, total, 0.0))
        total = jnp.where(slot == 0, total, jnp.concatenate([total[ROWS:], total[:ROWS]], axis=0))
        out_ref[d] = out_ref[d] + total


def receive_blocks(arrived_ref, count):
    slots = arrived_ref.shape[0] // ROWS
    onehot = arrived_ref[pl.ds(ROWS - 1, slots, stride=ROWS), :]
    fields = [arrived_ref[pl.ds(f, slots, stride=ROWS), :] for f in range(count)]
    return [
        lax.dot_general(
            onehot, field, (((0,), (0,)), ((), ())), precision=lax.Precision.HIGHEST, preferred_element_type=jnp.float32
        )
        for field in fields
    ]


def index_copies(refs, held_refs, sems):
    return [pltpu.make_async_copy(src, dst, sems.at[i]) for i, (src, dst) in enumerate(zip(refs, held_refs))]


def air_send_kernel(
    dest_hbm,
    source_hbm,
    window_hbm,
    arrived_ref,
    some_air_ref,
    weights_ref,
    out_ref,
    flux_ref,
    picked_ref,
    counts_ref,
    dest_ref,
    source_ref,
    window_ref,
    sems,
):
    indices = index_copies((dest_hbm, source_hbm, window_hbm), (dest_ref, source_ref, window_ref), sems)
    for copy in indices:
        copy.start()
    rows = some_air_ref.shape[2]
    surface = [some_air_ref[f, 0] for f in range(4)]
    on_air = [field[:rows] for field in receive_blocks(arrived_ref, 3)]
    relative_u = surface[2] - on_air[1]
    relative_v = surface[3] - on_air[2]
    wind_speed = jnp.sqrt(relative_u * relative_u + relative_v * relative_v + 1.0)
    flux_ref[0] = 0.5 * wind_speed * (on_air[0] - surface[0])
    flux_ref[1] = 0.4 * wind_speed * (0.8 * on_air[0] - surface[1])

    for copy in indices:
        copy.wait()

    def pick(k, f):
        return flux_ref[f, pl.ds(source_ref[k], 1), :]

    send_blocks(pick, 2, weights_ref, dest_ref, window_ref, picked_ref, counts_ref, out_ref)


def air_send(arrived, some_air, weights, dest, source, window):
    blocks = weights.shape[0]
    tiles = arrived.shape[0]
    vmem = pl.BlockSpec(memory_space=pltpu.VMEM)
    return pl.pallas_call(
        air_send_kernel,
        in_specs=[vmem] * 6,
        out_specs=(vmem, vmem),
        out_shape=(
            pltpu.VMEM((tiles, CAP * ROWS, WIN), jnp.float32),
            pltpu.VMEM((2,) + some_air.shape[2:], jnp.float32),
        ),
        scratch_shapes=[pltpu.VMEM((blocks, SUB, WIN), jnp.float32), pltpu.SMEM((tiles,), jnp.int32)]
        + [pltpu.SMEM((blocks,), jnp.int32)] * 3
        + [pltpu.SemaphoreType.DMA((3,))],
        compiler_params=pltpu.CompilerParams(vmem_limit_bytes=VMEM_LIMIT),
        cost_estimate=pl.CostEstimate(flops=blocks * 2 * 16 * 128 * 256, bytes_accessed=2000000, transcendentals=0),
        name="air_send",
    )(
        held(dest),
        held(source),
        held(window),
        held(arrived.reshape(tiles * CAP * ROWS, WIN)),
        some_air,
        held(weights),
    )


def sea_forcing_kernel(arrived_ref, land_ref, top_ref, before_ref, after_ref, summed_ref, new_ref, sem):
    del before_ref
    rows, cols = land_ref.shape
    halves = cols // WIN
    for f, field in enumerate(receive_blocks(arrived_ref, 2)):
        summed_ref[f] = field
        for h in range(halves):
            span = pl.ds(h * WIN, WIN)
            forcing = summed_ref[f, pl.ds(h, rows, stride=halves), :] * (-0.5, 0.3)[f]
            change = jnp.where(land_ref[:, span] == 1, time_step * forcing, 0.0)
            new_ref[f, :, span] = top_ref[f, :, span] + change
    copy = pltpu.make_async_copy(new_ref, after_ref.at[:, 0], sem)
    copy.start()
    copy.wait()


def add_sea_forcing(arrived, land, top, sea_next):
    tiles = arrived.shape[0]
    rows, cols = land.shape
    vmem = pl.BlockSpec(memory_space=pltpu.VMEM)
    hbm = pl.BlockSpec(memory_space=pltpu.HBM)
    return pl.pallas_call(
        sea_forcing_kernel,
        in_specs=[vmem, vmem, vmem, hbm],
        out_specs=hbm,
        out_shape=jax.ShapeDtypeStruct(sea_next.shape, jnp.float32),
        scratch_shapes=[
            pltpu.VMEM((2, rows * cols // WIN, WIN), jnp.float32),
            pltpu.VMEM((2, rows, cols), jnp.float32),
            pltpu.SemaphoreType.DMA(()),
        ],
        input_output_aliases={3: 0},
        compiler_params=pltpu.CompilerParams(vmem_limit_bytes=VMEM_LIMIT),
        cost_estimate=pl.CostEstimate(flops=4000000, bytes_accessed=600000, transcendentals=0),
        name="sea_forcing",
    )(held(arrived.reshape(tiles * CAP * ROWS, WIN)), held(land), top, sea_next)


def padded_levels(levels):
    return -(-levels // SUB) * SUB


CHUNKS = 4


def first_kernel(
    dest_hbm,
    source_hbm,
    window_hbm,
    atm_ref,
    ocean_ref,
    weights_ref,
    out_ref,
    first_ref,
    second_ref,
    y_ref,
    some_air_ref,
    air,
    sea,
    sea_v,
    low,
    high,
    low_u,
    high_u,
    weights,
    top,
    windows,
    picked,
    counts,
    dest_ref,
    source_ref,
    window_ref,
    sems,
    weight_sems,
    top_sems,
    index_sems,
):
    air_levels, air_rows = atm_ref.shape[1:3]
    sea_levels, sea_rows, sea_cols = ocean_ref.shape[1:]
    halves = sea_cols // WIN
    pitch = padded_levels(air_levels)
    gx, gy, last_gx = lax.axis_index("gx"), lax.axis_index("gy"), lax.axis_size("gx") - 1
    even = gx % 2 == 0
    at_end = (gx == 0) | (gx == last_gx)
    edge = jnp.where(gy == 0, LANES - 1, 0)
    near_half = jnp.where(gy == 0, 1, 0)
    span = pl.ds(pl.multiple_of(near_half * LANES, LANES), LANES)
    far = pl.ds(pl.multiple_of((1 - near_half) * LANES, LANES), LANES)
    a, o = air_levels // CHUNKS, sea_levels // CHUNKS

    tops = [pltpu.make_async_copy(ocean_ref.at[f, 0], top.at[i], top_sems.at[i]) for i, f in enumerate((0, 2, 3))]
    weights_in = pltpu.make_async_copy(weights_ref, weights, weight_sems)

    def copies(chunk):
        air_span, sea_span = pl.ds(chunk * a, a), pl.ds(chunk * o, o)
        pairs = [
            (atm_ref.at[:, air_span], air.at[:, air_span]),
            (ocean_ref.at[pl.ds(0, 2), sea_span, :, span], sea.at[:, sea_span]),
            (ocean_ref.at[3, sea_span, :, span], sea_v.at[sea_span]),
            (ocean_ref.at[pl.ds(0, 2), sea_span, pl.ds(0, SUB), far], low.at[:, sea_span]),
            (ocean_ref.at[pl.ds(0, 2), sea_span, pl.ds(sea_rows - SUB, SUB), far], high.at[:, sea_span]),
            (ocean_ref.at[2, sea_span, pl.ds(0, SUB)], low_u.at[sea_span]),
            (ocean_ref.at[2, sea_span, pl.ds(sea_rows - SUB, SUB)], high_u.at[sea_span]),
        ]
        return [pltpu.make_async_copy(src, dst, sems.at[chunk, i]) for i, (src, dst) in enumerate(pairs)]

    indices = index_copies((dest_hbm, source_hbm, window_hbm), (dest_ref, source_ref, window_ref), index_sems)
    for copy in indices + tops:
        copy.start()
    weights_in.start()
    for chunk in range(CHUNKS):
        for copy in copies(chunk):
            copy.start()

    for copy in indices + tops:
        copy.wait()
    for f in range(3):
        for h in range(halves):
            windows[f, pl.ds(h, sea_rows, stride=halves), :] = top[f, :, pl.ds(h * WIN, WIN)]
    weights_in.wait()

    def pick(k, f):
        return windows[f, pl.ds(source_ref[k], 1), :]

    send_blocks(pick, 3, weights, dest_ref, window_ref, picked, counts, out_ref)

    for f in range(3):
        for ref in (first_ref, second_ref):
            ref[pl.ds((f + 1) * pitch - SUB, SUB), :] = jnp.zeros((SUB, LANES), jnp.float32)

    def put_rows(to, low_row, high_row):
        first_ref[pl.ds(to, 1), :] = jnp.where(even, high_row, low_row)
        second_ref[pl.ds(to, 1), :] = jnp.where(at_end, 0.0, jnp.where(even, low_row, high_row))

    def put(total, column, to, lane):
        return jnp.where(lane == to, pltpu.roll(column, (to - edge + LANES) % LANES, 1), total)

    air_lane, sea_lane = lane_of((air_rows, LANES)), lane_of((sea_rows, LANES))
    tracers = v = jnp.zeros((air_rows, LANES), jnp.float32)
    total = jnp.zeros((sea_rows, LANES), jnp.float32)
    for chunk in range(CHUNKS):
        for copy in copies(chunk):
            copy.wait()
        if chunk == 0:
            some_air_ref[...] = air[:, : some_air_ref.shape[1]]
        for level in range(chunk * a, (chunk + 1) * a):
            tracers = put(tracers, air[0, level], level, air_lane)
            tracers = put(tracers, air[1, level], LANES // 2 + level, air_lane)
            v = put(v, air[3, level], level, air_lane)
            for f in range(3):
                put_rows(f * pitch + level, air[f, level, pl.ds(0, 1), :], air[f, level, pl.ds(air_rows - 1, 1), :])
        for level in range(chunk * o, (chunk + 1) * o):
            total = put(total, sea[0, level], level, sea_lane)
            total = put(total, sea[1, level], sea_levels + level, sea_lane)
            total = put(total, sea_v[level], 2 * sea_levels + level, sea_lane)
            at = 3 * pitch + level
            for f in range(2):
                near_rows = sea[f, level, pl.ds(0, 1), :], sea[f, level, pl.ds(sea_rows - 1, 1), :]
                far_rows = low[f, level, pl.ds(0, 1), :], high[f, level, pl.ds(SUB - 1, 1), :]
                put_rows(at + (f * halves + near_half) * sea_levels, *near_rows)
                put_rows(at + (f * halves + 1 - near_half) * sea_levels, *far_rows)
            for h in range(halves):
                tile = pl.ds(h * WIN, WIN)
                u_rows = low_u[level, pl.ds(0, 1), tile], high_u[level, pl.ds(SUB - 1, 1), tile]
                put_rows(at + (2 * halves + h) * sea_levels, *u_rows)
    y_ref[:air_rows] = tracers
    y_ref[air_rows : 2 * air_rows] = v
    y_ref[2 * air_rows :] = total


def first(tiles, atm, ocean, weights, dest, source, window):
    blocks = weights.shape[0]
    air_levels, air_rows, _ = atm.shape[1:]
    sea_levels, sea_rows, sea_cols = ocean.shape[1:]
    xrows = 3 * padded_levels(air_levels) + 3 * sea_levels * (sea_cols // WIN)
    yrows = 2 * air_rows + sea_rows
    vmem = pl.BlockSpec(memory_space=pltpu.VMEM)
    hbm = pl.BlockSpec(memory_space=pltpu.HBM)
    return pl.pallas_call(
        first_kernel,
        in_specs=[hbm] * 6,
        out_specs=[vmem] * 5,
        out_shape=(
            pltpu.VMEM((tiles, CAP * ROWS, WIN), jnp.float32),
            pltpu.VMEM((xrows, LANES), jnp.float32),
            pltpu.VMEM((xrows, LANES), jnp.float32),
            pltpu.VMEM((yrows, LANES), jnp.float32),
            pltpu.VMEM((4, air_levels // STEPS, air_rows, LANES), jnp.float32),
        ),
        scratch_shapes=[
            pltpu.VMEM(atm.shape, jnp.float32),
            pltpu.VMEM((2, sea_levels, sea_rows, LANES), jnp.float32),
            pltpu.VMEM((sea_levels, sea_rows, LANES), jnp.float32),
            pltpu.VMEM((2, sea_levels, SUB, LANES), jnp.float32),
            pltpu.VMEM((2, sea_levels, SUB, LANES), jnp.float32),
            pltpu.VMEM((sea_levels, SUB, sea_cols), jnp.float32),
            pltpu.VMEM((sea_levels, SUB, sea_cols), jnp.float32),
            pltpu.VMEM(weights.shape, jnp.float32),
            pltpu.VMEM((3, sea_rows, sea_cols), jnp.float32),
            pltpu.VMEM((3, sea_rows * sea_cols // WIN, WIN), jnp.float32),
            pltpu.VMEM((blocks, SUB, WIN), jnp.float32),
            pltpu.SMEM((tiles,), jnp.int32),
            pltpu.SMEM((blocks,), jnp.int32),
            pltpu.SMEM((blocks,), jnp.int32),
            pltpu.SMEM((blocks,), jnp.int32),
            pltpu.SemaphoreType.DMA((CHUNKS, 7)),
            pltpu.SemaphoreType.DMA(()),
            pltpu.SemaphoreType.DMA((3,)),
            pltpu.SemaphoreType.DMA((3,)),
        ],
        compiler_params=pltpu.CompilerParams(vmem_limit_bytes=VMEM_LIMIT),
        cost_estimate=pl.CostEstimate(flops=30000000, bytes_accessed=12000000, transcendentals=0),
        name="first",
    )(left(dest), left(source), left(window), left(atm), left(ocean), left(weights))


STEPS = 5
PAD = 8
SHIFTED = (3,)


def beyond_columns(gy, mine, v_mine, other, v_other):
    scale, mixing = 0.25 * time_step, time_step * diffusion
    sign = jnp.where(gy == 0, -scale, scale)
    return mixing * other + sign * ((v_mine + v_other) * other + v_other * mine)


def shift_matrix():
    shape = (2 * LANES, 2 * LANES)
    source, to = row_of(shape) % LANES, lane_of(shape)
    left = jnp.where(to < LANES, (to + 1) % LANES, (to + LANES - 1) % LANES)
    return jnp.where(source == left, 1.0, 0.0).astype(jnp.bfloat16)


def shifted_rows(rows, matrix):
    high = rows.astype(jnp.bfloat16)
    low = (rows - high.astype(jnp.float32)).astype(jnp.bfloat16)
    return jnp.dot(jnp.concatenate([high, low], axis=1), matrix, preferred_element_type=jnp.float32)


def step_level(ref, index, shifted, groups, halves, beyond, write):
    lane = lane_of((SUB, LANES))
    first_lane, last_lane = lane == 0, lane == LANES - 1
    scale, mixing = 0.25 * time_step, time_step * diffusion

    def rows(f, h, r, offset):
        return ref[index(f, h) + (pl.ds(PAD + r * SUB + offset, SUB), slice(None))]

    def along_y(f, r, tiles):
        if f in SHIFTED:
            left, right = zip(*[shifted(f, r, h) for h in range(halves)])
            left, right = list(left), list(right)
        else:
            right = [pltpu.roll(t, 1, 1) for t in tiles]
            left = [pltpu.roll(t, LANES - 1, 1) for t in tiles]
        lows = [jnp.where(first_lane, b, t) for b, t in zip([0.0] + right[:-1], right)]
        highs = [jnp.where(last_lane, b, t) for b, t in zip(left[1:] + [0.0], left)]
        return lows, highs

    for r in range(groups):
        q = [[rows(f, h, r, 0) for h in range(halves)] for f in range(2)]
        v = [scale * rows(3, h, r, 0) for h in range(halves)]
        v_low, v_high = along_y(3, r, v)
        sides = [along_y(f, r, q[f]) for f in range(2)]
        for h in range(halves):
            u, u_low, u_high = (scale * rows(2, h, r, offset) for offset in (0, -1, 1))
            centre = (1.0 - 4.0 * mixing) + ((u_low - u_high) + (v_low[h] - v_high[h]))
            x_high, x_low = (mixing - u) - u_high, (mixing + u) + u_low
            y_high, y_low = (mixing - v[h]) - v_high[h], (mixing + v[h]) + v_low[h]
            for f in range(2):
                new = centre * q[f][h] + (x_high * rows(f, h, r, 1) + x_low * rows(f, h, r, -1))
                new = new + (y_high * sides[f][1][h] + y_low * sides[f][0][h])
                write(f, r, h, new + beyond(f, r, h), q[f][h])


def transport_kernel(
    atm_ref,
    ocean_ref,
    some_air_ref,
    land_ref,
    flux_ref,
    first_ref,
    second_ref,
    mine_ref,
    y_ref,
    air_ref,
    sea_ref,
    top_ref,
    air,
    sea,
    air_new,
    sea_new,
    air_edge,
    sea_edge,
    air_shifted,
    sea_shifted,
    matrix,
    in_sems,
    out_sems,
):
    all_air, air_rows = atm_ref.shape[1:3]
    all_sea, sea_rows, sea_cols = ocean_ref.shape[1:]
    a, o = all_air // STEPS, all_sea // STEPS
    halves = sea_cols // LANES
    pitch = padded_levels(all_air)
    even, gy = lax.axis_index("gx") % 2 == 0, lax.axis_index("gy")

    def air_in(step):
        levels = pl.ds(step * a, a)
        yield pltpu.make_async_copy(
            atm_ref.at[:, levels], air.at[:, levels, pl.ds(PAD, air_rows)], in_sems.at[step, halves]
        )

    def sea_in(start, count, sem):
        levels = pl.ds(start, count)
        for h in range(halves):
            yield pltpu.make_async_copy(
                ocean_ref.at[:, levels, :, pl.ds(h * LANES, LANES)],
                sea.at[h, :, levels, pl.ds(PAD, sea_rows)],
                in_sems.at[sem, h],
            )

    def air_out(step):
        levels = pl.ds(step * a, a)
        return pltpu.make_async_copy(air_new.at[:, levels], air_ref.at[:, levels], out_sems.at[step, 0])

    def sea_out(step):
        levels = pl.ds(step * o, o)
        return pltpu.make_async_copy(sea_new.at[:, levels], sea_ref.at[:, levels], out_sems.at[step, 1])

    half = o // 2
    for copy in (*sea_in(0, half, 0), *sea_in(half, half, STEPS)):
        copy.start()
    for step in range(1, STEPS):
        for copy in (*sea_in(step * o, o, step), *air_in(step)):
            copy.start()
    matrix[...] = shift_matrix()
    air[:, :a, pl.ds(PAD, air_rows), :] = some_air_ref[...]

    lane = lane_of((air_rows, LANES))
    mine, other = mine_ref[:air_rows], y_ref[:air_rows]

    def twice(v):
        return jnp.where(lane < LANES // 2, v, pltpu.roll(v, LANES // 2, 1))

    v_mine, v_other = twice(mine_ref[air_rows : 2 * air_rows]), twice(y_ref[air_rows : 2 * air_rows])
    air_edge[...] = beyond_columns(gy, mine, v_mine, other, v_other)
    lane = lane_of((sea_rows, LANES))
    mine, other = mine_ref[2 * air_rows :], y_ref[2 * air_rows :]

    def both(columns):
        first, second = (pltpu.roll(columns, LANES - n * all_sea, 1) for n in (2, 1))
        return jnp.where(lane < all_sea, first, second)

    sea_edge[...] = beyond_columns(gy, mine, both(mine), other, both(other))

    edge = jnp.where(gy == 0, LANES - 1, 0)
    lane = lane_of((SUB, LANES))
    at_first, at_last = (lane == 0) & (gy != 0), (lane == LANES - 1) & (gy == 0)
    at_edge = lane == edge

    def column(ref, r, at):
        return pltpu.roll(ref[pl.ds(r * SUB, SUB), :], (edge - at + LANES) % LANES, 1)

    def x_rows(at):
        one, other = first_ref[pl.ds(at, 1), :], second_ref[pl.ds(at, 1), :]
        return jnp.where(even, other, one), jnp.where(even, one, other)

    def some_air(step):
        for j in range(a):
            level = step * a + j
            for f in range(3):
                before, after = x_rows(f * pitch + level)
                air[f, level, pl.ds(PAD - 1, 1), :] = before
                air[f, level, pl.ds(PAD + air_rows, 1), :] = after
        for i, f in enumerate(SHIFTED):
            rows = air[f, pl.ds(step * a, a), pl.ds(PAD, air_rows), :].reshape(a * air_rows, LANES)
            air_shifted[i] = shifted_rows((0.25 * time_step if f == 3 else 1.0) * rows, matrix[...])
        stores = []
        for j in range(a):
            level = step * a + j

            def beyond(f, r, h):
                return jnp.where(at_edge, column(air_edge, r, f * (LANES // 2) + level), 0.0)

            def shifted(f, r, h):
                rows = pl.ds(j * air_rows + r * SUB, SUB)
                i = SHIFTED.index(f)
                return air_shifted[i, rows, pl.ds(0, LANES)], air_shifted[i, rows, pl.ds(LANES, LANES)]

            def write(f, r, h, new, q):
                stores.append((f, level, pl.ds(r * SUB, SUB), new))

            step_level(air, lambda f, h: (f, level), shifted, air_rows // SUB, 1, beyond, write)
        for *place, new in stores:
            air_new[tuple(place)] = new

    def some_sea(start, count):
        for j in range(count):
            level = start + j
            for f in range(3):
                for h in range(halves):
                    before, after = x_rows(3 * pitch + (f * halves + h) * all_sea + level)
                    sea[h, f, level, pl.ds(PAD - 1, 1), :] = before
                    sea[h, f, level, pl.ds(PAD + sea_rows, 1), :] = after
        for i, f in enumerate(SHIFTED):
            for h in range(halves):
                rows = sea[h, f, pl.ds(start, count), pl.ds(PAD, sea_rows), :].reshape(count * sea_rows, LANES)
                sea_shifted[i, h, : count * sea_rows] = shifted_rows((0.25 * time_step if f == 3 else 1.0) * rows, matrix[...])
        stores = []
        for j in range(count):
            level = start + j
            columns = {}

            def beyond(f, r, h):
                if (f, r) not in columns:
                    columns[f, r] = column(sea_edge, r, f * all_sea + level)
                added = columns[f, r]
                if h == 0:
                    return jnp.where(at_first, added, 0.0)
                return jnp.where(at_last, added, 0.0) if h == halves - 1 else 0.0

            def shifted(f, r, h):
                rows = pl.ds(j * sea_rows + r * SUB, SUB)
                i = SHIFTED.index(f)
                return sea_shifted[i, h, rows, pl.ds(0, LANES)], sea_shifted[i, h, rows, pl.ds(LANES, LANES)]

            def write(f, r, h, new, q):
                rows, span = pl.ds(r * SUB, SUB), pl.ds(h * LANES, LANES)
                stores.append((f, level, rows, span, jnp.where(land_ref[rows, span] == 1, new, q)))

            step_level(sea, lambda f, h: (h, f, level), shifted, sea_rows // SUB, halves, beyond, write)
        for *place, new in stores:
            sea_new[tuple(place)] = new

    some_air(0)
    for f in range(2):
        air_new[f, 0] = air_new[f, 0] + time_step * flux_ref[f]
    air_out(0).start()

    for start, sem in ((0, 0), (half, STEPS)):
        for copy in sea_in(start, half, sem):
            copy.wait()
        some_sea(start, half)
    sea_out(0).start()
    top_ref[...] = sea_new[:, 0]

    def some_levels(step, carry):
        for copy in sea_in(step * o, o, step):
            copy.wait()
        some_sea(step * o, o)
        sea_out(step).start()
        for copy in air_in(step):
            copy.wait()
        some_air(step)
        air_out(step).start()
        return carry

    lax.fori_loop(1, STEPS, some_levels, 0)
    for step in range(STEPS):
        air_out(step).wait()
        sea_out(step).wait()


def transport(atm, ocean, some_air, land, flux, first_rows, second_rows, mine, y):
    air_levels, air_rows, _ = atm.shape[1:]
    sea_levels, sea_rows, sea_cols = ocean.shape[1:]
    halves = sea_cols // LANES
    vmem = pl.BlockSpec(memory_space=pltpu.VMEM)
    hbm = pl.BlockSpec(memory_space=pltpu.HBM)
    air_shape, sea_shape = (2,) + atm.shape[1:], (2,) + ocean.shape[1:]
    return pl.pallas_call(
        transport_kernel,
        in_specs=[hbm, hbm] + [vmem] * 7,
        out_specs=[hbm, hbm, vmem],
        out_shape=(
            jax.ShapeDtypeStruct(air_shape, jnp.float32),
            jax.ShapeDtypeStruct(sea_shape, jnp.float32),
            pltpu.VMEM((2, sea_rows, sea_cols), jnp.float32),
        ),
        scratch_shapes=[
            pltpu.VMEM((4, air_levels, air_rows + 2 * PAD, LANES), jnp.float32),
            pltpu.VMEM((halves, 4, sea_levels, sea_rows + 2 * PAD, LANES), jnp.float32),
            pltpu.VMEM(air_shape, jnp.float32),
            pltpu.VMEM(sea_shape, jnp.float32),
            pltpu.VMEM((air_rows, LANES), jnp.float32),
            pltpu.VMEM((sea_rows, LANES), jnp.float32),
            pltpu.VMEM((len(SHIFTED), air_levels // STEPS * air_rows, 2 * LANES), jnp.float32),
            pltpu.VMEM((len(SHIFTED), halves, sea_levels // STEPS * sea_rows, 2 * LANES), jnp.float32),
            pltpu.VMEM((2 * LANES, 2 * LANES), jnp.bfloat16),
            pltpu.SemaphoreType.DMA((STEPS + 1, halves + 1)),
            pltpu.SemaphoreType.DMA((STEPS, 2)),
        ],
        compiler_params=pltpu.CompilerParams(vmem_limit_bytes=VMEM_LIMIT),
        cost_estimate=pl.CostEstimate(flops=60000000, bytes_accessed=22000000, transcendentals=0),
        name="transport",
    )(left(atm), left(ocean), some_air, held(land), flux, held(first_rows), held(second_rows), mine, held(y))


def body(
    atm_fields,
    ocean_fields,
    land_sea,
    sea_weights,
    sea_dest,
    sea_source,
    sea_window,
    air_weights,
    air_dest,
    air_source,
    air_window,
):
    width_x, width_y = lax.axis_size("gx"), lax.axis_size("gy")
    assert width_y == 2 and width_x % 2 == 0 and ocean_fields.shape[3] == 2 * LANES
    tiles = width_x * width_y
    exchange = functools.partial(lax.all_to_all, axis_name=("gx", "gy"), split_axis=0, concat_axis=0, tiled=True)
    pairs = [(i, i ^ 1) for i in range(width_x)]
    other_pairs = [(i, i + 1 if i % 2 else i - 1) for i in range(1, width_x - 1)]

    to_air, rows, other_rows, mine, some_air = first(
        tiles, atm_fields, ocean_fields, sea_weights, sea_dest.reshape(-1), sea_source, sea_window
    )
    on_air = exchange(to_air)
    side = lax.ppermute(mine, "gy", [(0, 1), (1, 0)])
    rows = lax.ppermute(rows, "gx", pairs)
    other_rows = lax.ppermute(other_rows, "gx", other_pairs)
    to_sea, fluxes = air_send(on_air, some_air, air_weights, air_dest.reshape(-1), air_source, air_window)
    to_sea, side = lax.optimization_barrier((to_sea, side))
    on_sea = exchange(to_sea)
    air_next, sea_next, top = transport(
        atm_fields, ocean_fields, some_air, land_sea, fluxes, rows, other_rows, mine, side
    )
    sea_next = add_sea_forcing(on_sea, land_sea, top, sea_next)
    return (air_next, sea_next)


def solution(mesh):
    placed = (
        P("ens", None, "gx", "gy"),
        P("ens", None, "gx", "gy"),
        P(("ens", "gx"), "gy"),
        P(("ens", "gx", "gy"), None, None),
        P(("ens", "gx", "gy"), None),
        P(("ens", "gx", "gy")),
        P(("ens", "gx", "gy")),
        P(("ens", "gx", "gy"), None, None),
        P(("ens", "gx", "gy"), None),
        P(("ens", "gx", "gy")),
        P(("ens", "gx", "gy")),
    )
    return jax.shard_map(
        body,
        mesh=mesh,
        in_specs=placed,
        out_specs=(P("ens", None, "gx", "gy"), P("ens", None, "gx", "gy")),
        check_vma=False,
    )
```
